256 devices in a mesh: hit: 64 (over x, z, y_hi), conf: 4 (over y_lo, core).
Axes of the slice: x: 4, y: 4 (y_hi: 2, y_lo: 2; y = y_hi * 2 + y_lo), z: 8, core: 2. Of those that a mesh axis runs over, the one named last changes fastest.
Arguments:
- scores: bfloat16 [393216, 1024], P('hit', 'conf'), may hold values from -44 to 44, as said below
- conf_init: bfloat16 [1024, 256], P('conf'), may hold values from -0.625 to 0.625
Outputs:
- hit_factors: float32 [393216, 256], P(('hit', 'conf'))
- conf_factors: float32 [1024, 256], P('conf')
The draws below stay inside these ranges and needn't reach their ends.
Inputs may be any that keep to these rules, and one draw needn't show every extreme that they name: real-valued docking scores.
All inputs are finite; a program needn't handle non-finite values.
Results may differ from the reference program's by a relative error of at most 0.0015.
Values may be sent and summed in bfloat16 or wider, within the bound.
A program may use at most 64 MiB of HBM per device.

```python
import math
import jax
import jax.numpy as jnp
import numpy as np
from jax import lax

CONFS = 1024
R = 256
HITS = 393216


def conf_basis(key):
    key_basis = jax.random.fold_in(key, 21)
    return jax.random.randint(key_basis, (CONFS, R), -7, 8).astype(jnp.float32)


def sylvester_signs(order):
    sign_table = np.ones((1, 1), dtype=np.float32)
    for doubling in range(order.bit_length() - 1):
        sign_table = np.concatenate([np.concatenate([sign_table, sign_table], 1), np.concatenate([sign_table, -sign_table], 1)], 0)
    return sign_table


def draw_conf_init(key, part):
    basis = conf_basis(key)
    key = jax.random.fold_in(key, 5)
    column_scale = np.array([2.0 ** (-(8 * column // R)) for column in range(R)], dtype=np.float32)
    rotation = jnp.asarray(sylvester_signs(R))
    mixed = jnp.dot(basis * jnp.asarray(column_scale)[None, :], rotation, precision=lax.Precision.HIGHEST)
    factor = (100.0 / (18.667 * CONFS * R)) ** 0.5
    jitter = 0.002 * jax.random.normal(key, (CONFS, R), dtype=jnp.float32)
    return jnp.clip(mixed * factor + jitter, -0.625, 0.625).astype(jnp.bfloat16)


def draw_scores(key, part):
    basis = conf_basis(key)
    key_noise = jax.random.fold_in(key, 11)
    key_row = jax.random.fold_in(key, 12)
    key_col = jax.random.fold_in(key, 13)
    key_latent = jax.random.fold_in(key, 15)
    group_size = R // 32
    latent_count = R // 4
    latent_ids = np.arange(latent_count)
    tier_order = np.array([4, 3, 5, 2, 6, 1, 7, 0])
    latent_columns = tier_order[latent_ids // group_size] * (R // 8) + latent_ids % group_size
    latent_scale = np.array([2.0 ** (-(index // group_size)) for index in range(latent_count)], dtype=np.float32)
    latent_span = 1 + latent_ids % 7
    latent_coeffs = jax.random.randint(key_latent, (HITS, latent_count), jnp.asarray(-latent_span), jnp.asarray(latent_span + 1))
    chosen = jnp.take(basis, jnp.asarray(latent_columns), axis=1)
    weighted = latent_coeffs.astype(jnp.float32) * jnp.asarray(latent_scale)[None, :]
    low_rank = lax.dot_general(weighted, chosen, (((1,), (1,)), ((), ())), precision=lax.Precision.HIGHEST) * 0.02
    position = jnp.arange(HITS, dtype=jnp.float32) / HITS
    trend = jnp.exp(math.log(3.0) * (position - 0.5))
    row_scale = jnp.exp(jax.random.uniform(key_row, (HITS, 1), minval=math.log(0.3), maxval=math.log(3.0))) * trend[:, None]
    col_scale = jnp.exp(jax.random.uniform(key_col, (1, CONFS), minval=math.log(0.5), maxval=math.log(2.0)))
    base = jnp.clip(jax.random.normal(key_noise, (HITS, CONFS)), -4.0, 4.0) + low_rank
    return jnp.clip(base * row_scale * col_scale, -44.0, 44.0).astype(jnp.bfloat16)


def setup_inputs(seed: int = 0) -> dict:
    keys = jax.random.split(jax.random.key(seed), 3)
    return {
        "scores": draw_scores(jax.random.fold_in(keys[2], 71), 0),
        "conf_init": draw_conf_init(jax.random.fold_in(keys[2], 71), 0),
    }


def solve_right(rhs, gram, ridge_term):
    identity = jnp.eye(gram.shape[0], dtype=jnp.float32)
    factor = jnp.linalg.cholesky(gram + ridge_term * identity)
    halfway = jax.scipy.linalg.solve_triangular(factor, rhs.T, lower=True)
    return jax.scipy.linalg.solve_triangular(factor, halfway, lower=True, trans=1).T

def gram_of(matrix):
    return lax.dot_general(matrix.astype(jnp.float32), matrix.astype(jnp.float32), (((0,), (0,)), ((), ())), preferred_element_type=jnp.float32)

def reference(scores, conf_init):
    gram_conf = gram_of(conf_init)
    rhs_hit = jnp.dot(scores.astype(jnp.float32), conf_init.astype(jnp.float32), preferred_element_type=jnp.float32)
    hit_factors = solve_right(rhs_hit, gram_conf, 0.5)
    hit_rounded = hit_factors.astype(jnp.bfloat16)
    gram_hit = gram_of(hit_rounded)
    rhs_conf = lax.dot_general(scores.astype(jnp.float32), hit_rounded.astype(jnp.float32), (((0,), (0,)), ((), ())), preferred_element_type=jnp.float32)
    conf_factors = solve_right(rhs_conf, gram_hit, 0.5 * HITS)
    return (hit_factors, conf_factors)
```

```python
import jax
import jax.numpy as jnp
from jax import lax
from jax.experimental import pallas as pl
from jax.experimental.pallas import tpu as pltpu
from jax.sharding import PartitionSpec as P

MESH = pl.DeviceIdType.MESH
F32 = jnp.float32
BF16 = jnp.bfloat16
NX, NZ = 4, 8
CH = 256


def exact_dot(a, b):
    return jnp.dot(a, b, precision=lax.Precision.HIGHEST, preferred_element_type=F32)


def scaled_steps(low, count):
    scales = []
    for _ in range(count):
        scales.append(2.0 / (1.0 + low))
        low = 4.0 * low / (1.0 + low) ** 2
    return scales


class Inverse:
    def __init__(self, a, low, scaled, corrected):
        n = a.shape[0]
        rows = lax.broadcasted_iota(jnp.int32, (n, n), 0)
        cols = lax.broadcasted_iota(jnp.int32, (n, n), 1)
        self.eye = (rows == cols).astype(F32)
        self.unscale = 1.0 / jnp.sqrt(jnp.sum(a * a, axis=(0, 1), keepdims=True))
        self.a = a * self.unscale
        self.scales = scaled_steps(low, scaled)
        self.corrected = corrected
        s = self.scales[0]
        self.x = (2.0 * s) * self.eye - (s * s) * self.a
        self.y = (2.0 * s) * self.a - (s * s) * exact_dot(self.a, self.a)

    def run(self, first, last):
        for s in self.scales[first:last]:
            m = (2.0 * s) * self.eye - (s * s) * self.y
            self.x, self.y = exact_dot(self.x, m), exact_dot(self.y, m)

    def finish(self):
        x = self.x
        for _ in range(self.corrected):
            x = exact_dot(x, 2.0 * self.eye - exact_dot(self.a, x))
        return x * self.unscale


def kernel(
    ridge_conf,
    ridge_hit,
    scores,
    conf_init,
    hit_out,
    conf_out,
    s_buf,
    c_buf,
    z_buf,
    g_acc,
    t_acc,
    g_core,
    g_half,
    g_xy,
    g_z,
    g_full,
    t_core,
    t_y,
    r_x,
    r_part,
    r_zy,
    r_full,
    cs, cr, ss, sr, sl, os,
    g1s, g1r, g2s, g2r, g3s, g3r, g4s, g4r, g5s, g5r,
    h1s, h1r, h2s, h2r, h3s, h3r, h4s, h4r, h5s, h5r, h6s, h6r,
):
    own = s_buf.shape[1]
    chunks = own // CH
    hit = lax.axis_index("hit")
    conf = lax.axis_index("conf")
    x = hit // (2 * NZ)
    z = (hit // 2) % NZ
    yh = hit % 2
    yl = conf // 2
    core = conf % 2

    def device(x_, yh_, z_, yl_, core_):
        return ((x_ * NZ + z_) * 2 + yh_, yl_ * 2 + core_)

    plane = x * 4 + yh * 2 + yl
    column = z * 2 + yh

    def plane_peer(r):
        p = (plane + r) % 16
        return p, device(p // 4, (p // 2) % 2, z, p % 2, core)

    def z_peer(r):
        return device(x, yh, (z + r) % NZ, yl, core)

    def column_peer(r):
        p = (column + r) % 16
        return p, device(x, p % 2, p // 2, yl, core)

    def x_peer(r):
        p = (x + r) % NX
        return p, device(p, yh, z, yl, core)

    group_conf = [conf, yl * 2 + 1 - core, (1 - yl) * 2 + core, (1 - yl) * 2 + 1 - core]
    group = [(hit, c) for c in group_conf]

    barrier = pltpu.get_barrier_semaphore()

    def greet(to):
        pl.semaphore_signal(barrier, inc=1, device_id=to, device_id_type=MESH)

    greet(group[1])
    greet(group[3])

    @pl.loop(1, 16)
    def _(r):
        greet(plane_peer(r)[1])

    @pl.loop(1, NZ)
    def _(r):
        greet(z_peer(r))
        greet(device(x, 1 - yh, (z + r) % NZ, yl, core))

    pl.semaphore_wait(barrier, 2 + 15 + 2 * (NZ - 1))

    def send(src, dst, send_sem, recv_sem, to):
        copy = pltpu.make_async_remote_copy(
            src_ref=src, dst_ref=dst, send_sem=send_sem, recv_sem=recv_sem, device_id=to, device_id_type=MESH
        )
        return copy

    def rows(start, size):
        return pl.ds(pl.multiple_of(start, size), size)

    conf_copies = [send(conf_init, c_buf.at[d], cs.at[d], cr.at[d], group[d]) for d in (1, 2)]
    for copy in conf_copies:
        copy.start()

    def score_copy(d, i):
        return send(
            scores.at[rows(group_conf[d] * own + i * CH, CH)],
            s_buf.at[d, rows(i * CH, CH)],
            ss.at[d, i],
            sr.at[d, i],
            group[d],
        )

    mine = pltpu.make_async_copy(scores.at[rows(conf * own, own)], s_buf.at[0], sl.at[0])
    mine.start()

    @pl.loop(0, chunks)
    def _(i):
        for d in (2, 3, 1):
            score_copy(d, i).start()

    conf_copies[1].wait()
    passed_on = send(c_buf.at[2], c_buf.at[3], cs.at[3], cr.at[3], group[1])
    passed_on.start()
    conf_copies[0].wait()
    passed_on.wait()
    c_buf[0] = conf_init[...]

    def square(m):
        return lax.dot_general(m, m, (((0,), (0,)), ((), ())), preferred_element_type=F32)

    def ridged(gram, ridge):
        n = gram.shape[0]
        r_ = lax.broadcasted_iota(jnp.int32, (n, n), 0)
        c_ = lax.broadcasted_iota(jnp.int32, (n, n), 1)
        return gram + jnp.where(r_ == c_, F32(ridge), F32(0.0))

    gram_conf = (square(c_buf[0]) + square(c_buf[1])) + (square(c_buf[2]) + square(c_buf[3]))
    inverse = Inverse(ridged(gram_conf, ridge_conf), 4.8e-6, 11, 2)
    inverse.run(1, 11)
    g_full[...] = inverse.finish()

    g_acc[...] = jnp.zeros_like(g_acc)
    t_acc[...] = jnp.zeros_like(t_acc)
    mine.wait()

    def out_copy(i):
        part = rows(i * CH, CH)
        return pltpu.make_async_copy(z_buf.at[part], hit_out.at[part], os.at[i])

    @pl.loop(0, chunks)
    def _(i):
        part = rows(i * CH, CH)
        for d in (1, 2, 3):
            score_copy(d, i).wait()
        rhs = jnp.zeros((CH, 256), F32)
        for d in range(4):
            rhs += jnp.dot(s_buf[d, part, :], c_buf[d], preferred_element_type=F32)
        solved = exact_dot(rhs, g_full[...])
        z_buf[part, :] = solved
        out_copy(i).start()
        rounded = solved.astype(BF16)
        turned = solved.T.astype(BF16)
        g_acc[...] += jnp.dot(turned, rounded, preferred_element_type=F32)
        for d in range(4):
            t_acc[d] += jnp.dot(turned, s_buf[d, part, :], preferred_element_type=F32)

    half = rows(core * 128, 128)
    other_half = rows((1 - core) * 128, 128)
    g1 = send(g_acc.at[other_half], g_core, g1s.at[0], g1r.at[0], group[1])
    g1.start()
    h1 = [send(t_acc.at[2 * k + 1], t_core.at[k], h1s.at[k], h1r.at[k], group[1]) for k in (1, 0)]
    for copy in h1:
        copy.start()

    g1.wait()
    g_half[...] = g_acc[half, :] + g_core[...]

    def g2(r):
        p, to = plane_peer(r)
        return send(g_half.at[rows(p * 8, 8)], g_xy.at[r], g2s.at[r], g2r.at[r], to)

    @pl.loop(1, 16)
    def _(r):
        g2(r).start()

    h1[0].wait()
    t_acc[2] += t_core[1]
    h2 = send(t_acc.at[2], t_y, h2s.at[0], h2r.at[0], group[2])
    h2.start()
    h1[1].wait()
    t_acc[0] += t_core[0]

    g_xy[0] = g_half[rows(plane * 8, 8), :]

    @pl.loop(1, 16)
    def _(r):
        g2(r).wait()

    g_z[z] = jnp.sum(g_xy[...], axis=0)

    def g3(r):
        return send(g_z.at[z], g_z.at[z], g3s.at[r], g3r.at[r], z_peer(r))

    @pl.loop(1, NZ)
    def _(r):
        g3(r).start()

    @pl.loop(1, NZ)
    def _(r):
        g3(r).wait()

    kept = rows(core * 128 + plane * 8, 8)
    g_full[kept, :] = jnp.sum(g_z[...], axis=0)

    def g4(r):
        return send(g_full.at[kept], g_full.at[kept], g4s.at[r], g4r.at[r], plane_peer(r)[1])

    @pl.loop(1, 16)
    def _(r):
        g4(r).start()

    @pl.loop(1, 16)
    def _(r):
        g4(r).wait()

    g5 = send(g_full.at[half], g_full.at[half], g5s.at[0], g5r.at[0], group[1])
    g5.start()

    h2.wait()
    t_acc[0] += t_y[...]

    def h3(r):
        p, to = x_peer(r)
        return send(t_acc.at[0, rows(p * 64, 64)], r_x.at[r], h3s.at[r], h3r.at[r], to)

    for r in (1, 3, 2):
        h3(r).start()

    g5.wait()
    inverse = Inverse(ridged(g_full[...], ridge_hit), 4.9e-7, 12, 2)
    inverse.run(1, 3)

    for r in (1, 3, 2):
        h3(r).wait()
    r_part[...] = (t_acc[0, rows(x * 64, 64), :] + r_x[1]) + (r_x[2] + r_x[3])

    def h4(r):
        p, to = column_peer(r)
        return send(
            r_part.at[rows(p // 2 * 8, 8), rows(p % 2 * 128, 128)], r_zy.at[r], h4s.at[r], h4r.at[r], to
        )

    @pl.loop(1, 16)
    def _(r):
        h4(r).start()

    inverse.run(3, 6)

    r_zy[0] = r_part[rows(z * 8, 8), rows(yh * 128, 128)]

    @pl.loop(1, 16)
    def _(r):
        h4(r).wait()

    piece = (rows(x * 64 + z * 8, 8), rows(yh * 128, 128))
    r_full[piece] = jnp.sum(r_zy[...], axis=0)

    def h5(r):
        return send(r_full.at[piece], r_full.at[piece], h5s.at[r], h5r.at[r], column_peer(r)[1])

    @pl.loop(1, 16)
    def _(r):
        h5(r).start()

    inverse.run(6, 9)

    @pl.loop(1, 16)
    def _(r):
        h5(r).wait()

    def h6(r):
        block = rows(x * 64, 64)
        return send(r_full.at[block], r_full.at[block], h6s.at[r], h6r.at[r], x_peer(r)[1])

    for r in (1, 3, 2):
        h6(r).start()

    inverse.run(9, 12)
    solver = inverse.finish()

    for r in (1, 3, 2):
        h6(r).wait()
    conf_out[...] = exact_dot(r_full[...].T, solver)

    @pl.loop(0, chunks)
    def _(i):
        out_copy(i).wait()


def shards(scores, conf_init):
    hits, confs = scores.shape
    rank = conf_init.shape[1]
    own = hits // 4
    chunks = own // CH
    total_hits = hits * lax.axis_size("hit")
    vmem = pltpu.VMEM
    dma = pltpu.SemaphoreType.DMA

    def body(*refs):
        kernel(0.5, 0.5 * total_hits, *refs)

    return pl.pallas_call(
        body,
        out_shape=(
            jax.ShapeDtypeStruct((own, rank), F32),
            jax.ShapeDtypeStruct((confs, rank), F32),
        ),
        in_specs=[pl.BlockSpec(memory_space=pl.ANY), pl.BlockSpec(memory_space=pltpu.VMEM)],
        out_specs=(pl.BlockSpec(memory_space=pl.ANY), pl.BlockSpec(memory_space=pltpu.VMEM)),
        scratch_shapes=[
            vmem((4, own, confs), BF16),
            vmem((4, confs, rank), BF16),
            vmem((own, rank), F32),
            vmem((rank, rank), F32),
            vmem((4, rank, confs), F32),
            vmem((128, rank), F32),
            vmem((128, rank), F32),
            vmem((16, 8, rank), F32),
            vmem((NZ, 8, rank), F32),
            vmem((rank, rank), F32),
            vmem((2, rank, confs), F32),
            vmem((rank, confs), F32),
            vmem((NX, 64, confs), F32),
            vmem((64, confs), F32),
            vmem((16, 8, 128), F32),
            vmem((rank, confs), F32),
            dma((4,)), dma((4,)), dma((4, chunks)), dma((4, chunks)), dma((1,)), dma((chunks,)),
            dma((1,)), dma((1,)), dma((16,)), dma((16,)), dma((NZ,)), dma((NZ,)), dma((16,)), dma((16,)), dma((1,)), dma((1,)),
            dma((2,)), dma((2,)), dma((1,)), dma((1,)), dma((NX,)), dma((NX,)), dma((16,)), dma((16,)), dma((16,)), dma((16,)),
            dma((NX,)), dma((NX,)),
        ],
        compiler_params=pltpu.CompilerParams(
            collective_id=0, has_side_effects=True, vmem_limit_bytes=40 * 1024 * 1024
        ),
    )(scores, conf_init)


def solution(mesh):
    return jax.shard_map(
        shards,
        mesh=mesh,
        in_specs=(P("hit", "conf"), P("conf", None)),
        out_specs=(P(("hit", "conf"), None), P("conf", None)),
        check_vma=False,
    )
```

```python
import jax
import jax.numpy as jnp
from jax import lax
from jax.experimental import pallas as pl
from jax.experimental.pallas import tpu as pltpu
from jax.sharding import PartitionSpec as P

MESH = pl.DeviceIdType.MESH
F32 = jnp.float32
BF16 = jnp.bfloat16
NX, NZ = 4, 8
CH = 128


def exact_dot(a, b):
    return jnp.dot(a, b, precision=lax.Precision.HIGHEST, preferred_element_type=F32)


def split(a):
    high = a.astype(BF16)
    return high, (a - high.astype(F32)).astype(BF16)


def split_dot(a, b):
    (ah, al), (bh, bl) = a, b
    one = lambda u, v: jnp.dot(u, v, preferred_element_type=F32)
    return one(ah, bl) + one(al, bh) + one(ah, bh)


def scaled_steps(low, count):
    scales = []
    for _ in range(count):
        scales.append(2.0 / (1.0 + low))
        low = 4.0 * low / (1.0 + low) ** 2
    return scales


class Inverse:
    def __init__(self, a, low, scaled, corrected):
        n = a.shape[0]
        rows = lax.broadcasted_iota(jnp.int32, (n, n), 0)
        cols = lax.broadcasted_iota(jnp.int32, (n, n), 1)
        self.eye = (rows == cols).astype(F32)
        self.unscale = 1.0 / jnp.sqrt(jnp.sum(a * a, axis=(0, 1), keepdims=True))
        self.a = a * self.unscale
        self.scales = scaled_steps(low, scaled)
        self.corrected = corrected
        s = self.scales[0]
        halves = split(self.a)
        self.x = (2.0 * s) * self.eye - (s * s) * self.a
        self.y = (2.0 * s) * self.a - (s * s) * split_dot(halves, halves)

    def run(self, first, last):
        for s in self.scales[first:last]:
            m = split((2.0 * s) * self.eye - (s * s) * self.y)
            self.x, self.y = split_dot(split(self.x), m), split_dot(split(self.y), m)

    def finish(self):
        x = self.x
        for _ in range(self.corrected):
            x = x + split_dot(split(x), split(self.eye - exact_dot(self.a, x)))
        return x * self.unscale


def kernel(
    ridge_conf,
    ridge_hit,
    scores,
    conf_init,
    hit_out,
    conf_out,
    s_buf,
    c_buf,
    z_buf,
    g_acc,
    t_acc,
    g_core,
    g_half,
    g_xy,
    g_z,
    g_full,
    t_core,
    t_xz,
    t_piece,
    t_y,
    t_full,
    known,
    cs, cr, ss, sr, sl, os,
    g1s, g1r, g2s, g2r, g3s, g3r, g4s, g4r,
    h1s, h1r, h2s, h2r, h3s, h3r, h4s, h4r,
):
    own = s_buf.shape[1]
    chunks = own // CH
    hit = lax.axis_index("hit")
    conf = lax.axis_index("conf")
    x = hit // (2 * NZ)
    z = (hit // 2) % NZ
    yh = hit % 2
    yl = conf // 2
    core = conf % 2

    def device(x_, yh_, z_, yl_, core_):
        return ((x_ * NZ + z_) * 2 + yh_, yl_ * 2 + core_)

    y = yh * 2 + yl
    xy = x * 4 + y
    xz = x * NZ + z

    def along_x(r):
        return device((x + r) % NX, yh, z, yl, core)

    def along_y(r):
        p = (y + r) % 4
        return device(x, p // 2, z, p % 2, core)

    def along_z(r):
        return device(x, yh, (z + r) % NZ, yl, core)

    def xy_peer(r, core_):
        p = (xy + r) % 16
        return p, device(p // 4, (p // 2) % 2, z, p % 2, core_)

    def xz_peer(r):
        p = (xz + r) % 32
        return p, device(p // NZ, yh, p % NZ, yl, core)

    group_conf = [conf, yl * 2 + 1 - core, (1 - yl) * 2 + core, (1 - yl) * 2 + 1 - core]
    group = [(hit, c) for c in group_conf]
    beyond = device(x, 1 - yh, z, 1 - yl, core)

    barrier = pltpu.get_barrier_semaphore()
    neighbours = [along_x(1), along_x(3), along_y(1), along_y(3), along_z(1), along_z(NZ - 1)]
    for to in [group[1], group[3]] + neighbours:
        pl.semaphore_signal(barrier, inc=1, device_id=to, device_id_type=MESH)
    pl.semaphore_wait(barrier, 8)

    def tell(k, devices):
        for to in devices:
            pl.semaphore_signal(known.at[k], inc=1, device_id=to, device_id_type=MESH)

    def send(src, dst, send_sem, recv_sem, to):
        return pltpu.make_async_remote_copy(
            src_ref=src, dst_ref=dst, send_sem=send_sem, recv_sem=recv_sem, device_id=to, device_id_type=MESH
        )

    def rows(start, size):
        return pl.ds(pl.multiple_of(start, size), size)

    conf_copies = [send(conf_init, c_buf.at[d], cs.at[d], cr.at[d], to) for d, to in ((1, group[1]), (2, beyond))]
    for copy in conf_copies:
        copy.start()

    def score_copy(d, i):
        return send(
            scores.at[rows(group_conf[d] * own + i * CH, CH)],
            s_buf.at[d, rows(i * CH, CH)],
            ss.at[d, i],
            sr.at[d, i],
            group[d],
        )

    @pl.loop(0, chunks)
    def _(i):
        for d in (2, 3, 1):
            score_copy(d, i).start()

    mine = pltpu.make_async_copy(scores.at[rows(conf * own, own)], s_buf.at[0], sl.at[0])
    mine.start()

    tell(0, neighbours)

    conf_copies[1].wait()
    passed_on = send(c_buf.at[2], c_buf.at[3], cs.at[3], cr.at[3], group[1])
    passed_on.start()
    conf_copies[0].wait()
    c_buf[0] = conf_init[...]
    passed_on.wait()

    def square(m):
        return lax.dot_general(m, m, (((0,), (0,)), ((), ())), preferred_element_type=F32)

    def ridged(gram, ridge):
        n = gram.shape[0]
        r_ = lax.broadcasted_iota(jnp.int32, (n, n), 0)
        c_ = lax.broadcasted_iota(jnp.int32, (n, n), 1)
        return gram + jnp.where(r_ == c_, F32(ridge), F32(0.0))

    gram_conf = (square(c_buf[0]) + square(c_buf[1])) + (square(c_buf[2]) + square(c_buf[3]))
    inverse = Inverse(ridged(gram_conf, ridge_conf), 4.8e-6, 11, 2)
    inverse.run(1, 11)
    g_full[...] = inverse.finish()

    pl.semaphore_wait(known.at[0], 6)
    tell(1, [along_z(2), along_z(NZ - 2)])

    g_acc[...] = jnp.zeros_like(g_acc)
    t_acc[...] = jnp.zeros_like(t_acc)
    mine.wait()

    pl.semaphore_wait(known.at[1], 2)
    tell(2, [along_x(r) for r in (1, 2, 3)])
    pl.semaphore_wait(known.at[2], 3)
    tell(3, [group[1]])
    pl.semaphore_wait(known.at[3], 1)

    def out_copy(i):
        part = rows(i * CH, CH)
        return pltpu.make_async_copy(z_buf.at[part], hit_out.at[part], os.at[i])

    def solve_chunk(i):
        part = rows(i * CH, CH)
        for d in (1, 2, 3):
            score_copy(d, i).wait()
        rhs = jnp.zeros((CH, 256), F32)
        for d in range(4):
            rhs += jnp.dot(s_buf[d, part, :], c_buf[d], preferred_element_type=F32)
        solved = exact_dot(rhs, g_full[...])
        z_buf[part, :] = solved
        out_copy(i).start()
        turned = solved.T.astype(BF16)
        g_acc[...] += jnp.dot(turned, solved.astype(BF16), preferred_element_type=F32)
        return turned

    def add_cross(i, turned):
        part = rows(i * CH, CH)
        for d in range(4):
            t_acc[d % 2, d // 2] += jnp.dot(turned, s_buf[d, part, :], preferred_element_type=F32)

    @pl.loop(0, chunks - 1)
    def _(i):
        add_cross(i, solve_chunk(i))

    turned = solve_chunk(chunks - 1)

    half = rows(core * 128, 128)
    other_half = rows((1 - core) * 128, 128)
    g1 = send(g_acc.at[other_half], g_core, g1s.at[0], g1r.at[0], group[1])
    g1.start()

    add_cross(chunks - 1, turned)
    h1 = send(t_acc.at[1], t_core, h1s.at[0], h1r.at[0], group[1])
    h1.start()

    g1.wait()
    g_half[...] = g_acc[half, :] + g_core[...]

    def g2(r):
        p, to = xy_peer(r, core)
        return send(g_half.at[rows(p * 8, 8)], g_xy.at[r], g2s.at[r], g2r.at[r], to)

    @pl.loop(1, 16)
    def _(r):
        g2(r).start()

    h1.wait()
    t_acc[0] += t_core[...]

    def h2(r):
        p, to = xz_peer(r)
        return send(t_acc.at[0, :, rows(p * 8, 8)], t_xz.at[r], h2s.at[r], h2r.at[r], to)

    @pl.loop(1, 32)
    def _(r):
        h2(r).start()

    g_xy[0] = g_half[rows(xy * 8, 8), :]

    @pl.loop(1, 16)
    def _(r):
        g2(r).wait()

    g_z[z] = jnp.sum(g_xy[...], axis=0)

    def g3(r):
        return send(g_z.at[z], g_z.at[z], g3s.at[r], g3r.at[r], along_z(r))

    @pl.loop(1, NZ)
    def _(r):
        g3(r).start()

    @pl.loop(1, NZ)
    def _(r):
        g3(r).wait()

    kept = rows(core * 128 + xy * 8, 8)
    g_full[kept, :] = jnp.sum(g_z[...], axis=0)

    def g4(r, other):
        to = xy_peer(r, 1 - core if other else core)[1]
        return send(g_full.at[kept], g_full.at[kept], g4s.at[other, r], g4r.at[other, r], to)

    @pl.loop(1, 16)
    def _(r):
        g4(r, 0).start()
        g4(r, 1).start()

    g4(0, 1).start()

    @pl.loop(1, 32)
    def _(r):
        h2(r).wait()

    own_tile = rows(xz * 8, 8)
    t_xz[0] = t_acc[0, :, own_tile, :]
    t_piece[...] = jnp.sum(t_xz[...], axis=0)

    h3 = [
        send(t_piece.at[k], t_y.at[n], h3s.at[n], h3r.at[n], to)
        for n, (k, to) in enumerate([(0, device(x, 1 - yh, z, yl, core)), (1, group[2]), (1, beyond)])
    ]
    for copy in h3:
        copy.start()

    g4(0, 1).wait()

    @pl.loop(1, 16)
    def _(r):
        g4(r, 0).wait()
        g4(r, 1).wait()

    inverse = Inverse(ridged(g_full[...], ridge_hit), 4.9e-7, 12, 2)

    for copy in h3:
        copy.wait()
    t_full[own_tile, :] = (t_piece[0] + t_y[1]) + (t_y[0] + t_y[2])

    def h4(r):
        return send(t_full.at[own_tile], t_full.at[own_tile], h4s.at[r], h4r.at[r], xz_peer(r)[1])

    @pl.loop(1, 32)
    def _(r):
        h4(r).start()

    inverse.run(1, 12)
    solver = inverse.finish()

    @pl.loop(1, 32)
    def _(r):
        h4(r).wait()

    conf_out[...] = split_dot(split(t_full[...].T), split(solver))

    @pl.loop(0, chunks)
    def _(i):
        out_copy(i).wait()


def shards(scores, conf_init):
    hits, confs = scores.shape
    rank = conf_init.shape[1]
    own = hits // 4
    chunks = own // CH
    total_hits = hits * lax.axis_size("hit")
    vmem = pltpu.VMEM
    dma = pltpu.SemaphoreType.DMA

    def body(*refs):
        kernel(0.5, 0.5 * total_hits, *refs)

    return pl.pallas_call(
        body,
        out_shape=(
            jax.ShapeDtypeStruct((own, rank), F32),
            jax.ShapeDtypeStruct((confs, rank), F32),
        ),
        in_specs=[pl.BlockSpec(memory_space=pl.ANY), pl.BlockSpec(memory_space=pltpu.VMEM)],
        out_specs=(pl.BlockSpec(memory_space=pl.ANY), pl.BlockSpec(memory_space=pltpu.VMEM)),
        scratch_shapes=[
            vmem((4, own, confs), BF16),
            vmem((4, confs, rank), BF16),
            vmem((own, rank), F32),
            vmem((rank, rank), F32),
            vmem((2, 2, rank, confs), F32),
            vmem((128, rank), F32),
            vmem((128, rank), F32),
            vmem((16, 8, rank), F32),
            vmem((NZ, 8, rank), F32),
            vmem((rank, rank), F32),
            vmem((2, rank, confs), F32),
            vmem((32, 2, 8, confs), F32),
            vmem((2, 8, confs), F32),
            vmem((3, 8, confs), F32),
            vmem((rank, confs), F32),
            pltpu.SemaphoreType.REGULAR((4,)),
            dma((4,)), dma((4,)), dma((4, chunks)), dma((4, chunks)), dma((1,)), dma((chunks,)),
            dma((1,)), dma((1,)), dma((16,)), dma((16,)), dma((NZ,)), dma((NZ,)), dma((2, 16)), dma((2, 16)),
            dma((1,)), dma((1,)), dma((32,)), dma((32,)), dma((3,)), dma((3,)), dma((32,)), dma((32,)),
        ],
        compiler_params=pltpu.CompilerParams(
            collective_id=0, has_side_effects=True, vmem_limit_bytes=60 * 1024 * 1024
        ),
    )(scores, conf_init)


def solution(mesh):
    return jax.shard_map(
        shards,
        mesh=mesh,
        in_specs=(P("hit", "conf"), P("conf", None)),
        out_specs=(P(("hit", "conf"), None), P("conf", None)),
        check_vma=False,
    )
```

```python
import jax
import jax.numpy as jnp
from jax import lax
from jax.experimental import pallas as pl
from jax.experimental.pallas import tpu as pltpu
from jax.sharding import PartitionSpec as P

MESH = pl.DeviceIdType.MESH
F32 = jnp.float32
BF16 = jnp.bfloat16
NX, NZ = 4, 8
CH = 128


def exact_dot(a, b):
    return jnp.dot(a, b, precision=lax.Precision.HIGHEST, preferred_element_type=F32)


def split(a):
    high = a.astype(BF16)
    return high, (a - high.astype(F32)).astype(BF16)


def split_dot(a, b):
    (ah, al), (bh, bl) = a, b
    one = lambda u, v: jnp.dot(u, v, preferred_element_type=F32)
    return one(ah, bl) + one(al, bh) + one(ah, bh)


def scaled_steps(low, count):
    scales = []
    for _ in range(count):
        scales.append(2.0 / (1.0 + low))
        low = 4.0 * low / (1.0 + low) ** 2
    return scales


class Inverse:
    def __init__(self, a, low, scaled, corrected):
        n = a.shape[0]
        rows = lax.broadcasted_iota(jnp.int32, (n, n), 0)
        cols = lax.broadcasted_iota(jnp.int32, (n, n), 1)
        self.eye = (rows == cols).astype(F32)
        self.unscale = 1.0 / jnp.sqrt(jnp.sum(a * a, axis=(0, 1), keepdims=True))
        self.a = a * self.unscale
        self.scales = scaled_steps(low, scaled)
        self.corrected = corrected
        s = self.scales[0]
        halves = split(self.a)
        self.x = (2.0 * s) * self.eye - (s * s) * self.a
        self.y = (2.0 * s) * self.a - (s * s) * split_dot(halves, halves)

    def run(self, first, last):
        for s in self.scales[first:last]:
            m = split((2.0 * s) * self.eye - (s * s) * self.y)
            self.x, self.y = split_dot(split(self.x), m), split_dot(split(self.y), m)

    def finish(self):
        x = self.x
        for _ in range(self.corrected):
            x = x + split_dot(split(x), split(self.eye - exact_dot(self.a, x)))
        return x * self.unscale


def kernel(
    ridge_conf,
    ridge_hit,
    scores,
    conf_init,
    hit_out,
    conf_out,
    s_buf,
    c_buf,
    z_buf,
    g_acc,
    t_acc,
    g_core,
    g_half,
    g_xy,
    g_z,
    g_full,
    t_core,
    t_xy,
    t_part,
    t_z,
    t_full,
    known,
    cs, cr, ss, sr, sl, os,
    g1s, g1r, g2s, g2r, g3s, g3r, g4s, g4r, g5s, g5r,
    h1s, h1r, h2s, h2r, h3s, h3r, h4s, h4r, h5s, h5r,
):
    own = s_buf.shape[1]
    chunks = own // CH
    hit = lax.axis_index("hit")
    conf = lax.axis_index("conf")
    x = hit // (2 * NZ)
    z = (hit // 2) % NZ
    yh = hit % 2
    yl = conf // 2
    core = conf % 2

    def device(x_, yh_, z_, yl_, core_):
        return ((x_ * NZ + z_) * 2 + yh_, yl_ * 2 + core_)

    y = yh * 2 + yl
    xy = x * 4 + y

    def along_x(r):
        return device((x + r) % NX, yh, z, yl, core)

    def along_y(r):
        p = (y + r) % 4
        return device(x, p // 2, z, p % 2, core)

    def along_z(r):
        return device(x, yh, (z + r) % NZ, yl, core)

    def xy_peer(r):
        p = (xy + r) % 16
        return p, device(p // 4, (p // 2) % 2, z, p % 2, core)

    group_conf = [conf, yl * 2 + 1 - core, (1 - yl) * 2 + core, (1 - yl) * 2 + 1 - core]
    group = [(hit, c) for c in group_conf]
    beyond = device(x, 1 - yh, z, 1 - yl, core)

    barrier = pltpu.get_barrier_semaphore()
    neighbours = [along_x(1), along_x(3), along_y(1), along_y(3), along_z(1), along_z(NZ - 1)]
    for to in [group[1], group[3]] + neighbours:
        pl.semaphore_signal(barrier, inc=1, device_id=to, device_id_type=MESH)
    pl.semaphore_wait(barrier, 8)

    def tell(k, devices):
        for to in devices:
            pl.semaphore_signal(known.at[k], inc=1, device_id=to, device_id_type=MESH)

    def send(src, dst, send_sem, recv_sem, to):
        return pltpu.make_async_remote_copy(
            src_ref=src, dst_ref=dst, send_sem=send_sem, recv_sem=recv_sem, device_id=to, device_id_type=MESH
        )

    def rows(start, size):
        return pl.ds(pl.multiple_of(start, size), size)

    conf_copies = [send(conf_init, c_buf.at[d], cs.at[d], cr.at[d], to) for d, to in ((1, group[1]), (2, beyond))]
    for copy in conf_copies:
        copy.start()

    def score_copy(d, i):
        return send(
            scores.at[rows(group_conf[d] * own + i * CH, CH)],
            s_buf.at[d, rows(i * CH, CH)],
            ss.at[d, i],
            sr.at[d, i],
            group[d],
        )

    @pl.loop(0, chunks)
    def _(i):
        for d in (2, 3, 1):
            score_copy(d, i).start()

    mine = pltpu.make_async_copy(scores.at[rows(conf * own, own)], s_buf.at[0], sl.at[0])
    mine.start()

    tell(0, neighbours)

    conf_copies[1].wait()
    passed_on = send(c_buf.at[2], c_buf.at[3], cs.at[3], cr.at[3], group[1])
    passed_on.start()
    conf_copies[0].wait()
    c_buf[0] = conf_init[...]
    passed_on.wait()

    def square(m):
        return lax.dot_general(m, m, (((0,), (0,)), ((), ())), preferred_element_type=F32)

    def ridged(gram, ridge):
        n = gram.shape[0]
        r_ = lax.broadcasted_iota(jnp.int32, (n, n), 0)
        c_ = lax.broadcasted_iota(jnp.int32, (n, n), 1)
        return gram + jnp.where(r_ == c_, F32(ridge), F32(0.0))

    gram_conf = (square(c_buf[0]) + square(c_buf[1])) + (square(c_buf[2]) + square(c_buf[3]))
    inverse = Inverse(ridged(gram_conf, ridge_conf), 4.8e-6, 11, 2)
    inverse.run(1, 11)
    g_full[...] = inverse.finish()

    pl.semaphore_wait(known.at[0], 6)
    tell(1, [along_z(2), along_z(NZ - 2)])

    g_acc[...] = jnp.zeros_like(g_acc)
    t_acc[...] = jnp.zeros_like(t_acc)
    mine.wait()

    pl.semaphore_wait(known.at[1], 2)
    tell(2, [along_x(r) for r in (1, 2, 3)])
    pl.semaphore_wait(known.at[2], 3)

    def out_copy(i):
        part = rows(i * CH, CH)
        return pltpu.make_async_copy(z_buf.at[part], hit_out.at[part], os.at[i])

    def solve_chunk(i):
        part = rows(i * CH, CH)
        for d in (1, 2, 3):
            score_copy(d, i).wait()
        rhs = jnp.zeros((CH, 256), F32)
        for d in range(4):
            rhs += jnp.dot(s_buf[d, part, :], c_buf[d], preferred_element_type=F32)
        solved = exact_dot(rhs, g_full[...])
        z_buf[part, :] = solved
        out_copy(i).start()
        turned = solved.T.astype(BF16)
        g_acc[...] += jnp.dot(turned, solved.astype(BF16), preferred_element_type=F32)
        return turned

    def add_cross(i, turned):
        part = rows(i * CH, CH)
        for d in range(4):
            t_acc[d % 2, d // 2] += jnp.dot(turned, s_buf[d, part, :], preferred_element_type=F32)

    @pl.loop(0, chunks - 1)
    def _(i):
        add_cross(i, solve_chunk(i))

    turned = solve_chunk(chunks - 1)

    half = rows(core * 128, 128)
    other_half = rows((1 - core) * 128, 128)
    g1 = send(g_acc.at[other_half], g_core, g1s.at[0], g1r.at[0], group[1])
    g1.start()

    add_cross(chunks - 1, turned)
    h1 = send(t_acc.at[1], t_core, h1s.at[0], h1r.at[0], group[1])
    h1.start()

    g1.wait()
    g_half[...] = g_acc[half, :] + g_core[...]

    def g2(r):
        p, to = xy_peer(r)
        return send(g_half.at[rows(p * 8, 8)], g_xy.at[r], g2s.at[r], g2r.at[r], to)

    @pl.loop(1, 16)
    def _(r):
        g2(r).start()

    h1.wait()
    t_acc[0] += t_core[...]

    def h2(r):
        p, to = xy_peer(r)
        block, part = (p + yl) % 2, p // 4 * 2 + p // 2 % 2
        return send(t_acc.at[0, block, rows(part * 32, 32)], t_xy.at[r], h2s.at[r], h2r.at[r], to)

    @pl.loop(1, 16)
    def _(r):
        h2(r).start()

    g_xy[0] = g_half[rows(xy * 8, 8), :]

    @pl.loop(1, 16)
    def _(r):
        g2(r).wait()

    g_z[z] = jnp.sum(g_xy[...], axis=0)

    def g3(r):
        return send(g_z.at[z], g_z.at[z], g3s.at[r], g3r.at[r], along_z(r))

    @pl.loop(1, NZ)
    def _(r):
        g3(r).start()

    @pl.loop(1, NZ)
    def _(r):
        g3(r).wait()

    def g_rows(p):
        return rows(core * 128 + p * 8, 8)

    g_full[g_rows(xy), :] = jnp.sum(g_z[...], axis=0)

    def g4(r):
        return send(g_full.at[g_rows(xy)], g_full.at[g_rows(xy)], g4s.at[r], g4r.at[r], xy_peer(r)[1])

    def g5(r):
        part = g_rows((xy - r + 16) % 16)
        return send(g_full.at[part], g_full.at[part], g5s.at[r], g5r.at[r], group[1])

    @pl.loop(1, 16)
    def _(r):
        g4(r).start()

    g5(0).start()

    @pl.loop(1, 16)
    def _(r):
        h2(r).wait()

    part = x * 2 + yh
    own_rows = rows(part * 32, 32)
    t_xy[0] = t_acc[0, 0, own_rows, :]
    t_part[...] = jnp.sum(t_xy[...], axis=0)

    def h3(r):
        p = (z + r) % NZ
        tile = t_part.at[rows(p // 2 * 8, 8), rows(p % 2 * 128, 128)]
        return send(tile, t_z.at[r], h3s.at[r], h3r.at[r], along_z(r))

    @pl.loop(1, NZ)
    def _(r):
        h3(r).start()

    @pl.loop(1, 16)
    def _(r):
        g4(r).wait()
        g5(r).start()

    t_z[0] = t_part[rows(z // 2 * 8, 8), rows(z % 2 * 128, 128)]

    @pl.loop(1, NZ)
    def _(r):
        h3(r).wait()

    own_tile = (rows(part * 32 + z // 2 * 8, 8), rows(z % 2 * 128, 128))
    t_full[own_tile] = jnp.sum(t_z[...], axis=0)

    def h4(r):
        return send(t_full.at[own_tile], t_full.at[own_tile], h4s.at[r], h4r.at[r], along_z(r))

    @pl.loop(1, NZ)
    def _(r):
        h4(r).start()

    @pl.loop(0, 16)
    def _(r):
        g5(r).wait()

    inverse = Inverse(ridged(g_full[...], ridge_hit), 4.9e-7, 12, 2)
    inverse.run(1, 6)

    @pl.loop(1, NZ)
    def _(r):
        h4(r).wait()

    def h5(r):
        p = (part + r) % 8
        to = device(p // 2, p % 2, z, yl, core)
        return send(t_full.at[own_rows], t_full.at[own_rows], h5s.at[r], h5r.at[r], to)

    @pl.loop(1, 8)
    def _(r):
        h5(r).start()

    inverse.run(6, 12)
    solver = inverse.finish()

    @pl.loop(1, 8)
    def _(r):
        h5(r).wait()

    conf_out[...] = split_dot(split(t_full[...].T), split(solver))

    @pl.loop(0, chunks)
    def _(i):
        out_copy(i).wait()


def shards(scores, conf_init):
    hits, confs = scores.shape
    rank = conf_init.shape[1]
    own = hits // 4
    chunks = own // CH
    total_hits = hits * lax.axis_size("hit")
    vmem = pltpu.VMEM
    dma = pltpu.SemaphoreType.DMA

    def body(*refs):
        kernel(0.5, 0.5 * total_hits, *refs)

    return pl.pallas_call(
        body,
        out_shape=(
            jax.ShapeDtypeStruct((own, rank), F32),
            jax.ShapeDtypeStruct((confs, rank), F32),
        ),
        in_specs=[pl.BlockSpec(memory_space=pl.ANY), pl.BlockSpec(memory_space=pltpu.VMEM)],
        out_specs=(pl.BlockSpec(memory_space=pl.ANY), pl.BlockSpec(memory_space=pltpu.VMEM)),
        scratch_shapes=[
            vmem((4, own, confs), BF16),
            vmem((4, confs, rank), BF16),
            vmem((own, rank), F32),
            vmem((rank, rank), F32),
            vmem((2, 2, rank, confs), F32),
            vmem((128, rank), F32),
            vmem((128, rank), F32),
            vmem((16, 8, rank), F32),
            vmem((NZ, 8, rank), F32),
            vmem((rank, rank), F32),
            vmem((2, rank, confs), F32),
            vmem((16, 32, confs), F32),
            vmem((32, confs), F32),
            vmem((NZ, 8, 128), F32),
            vmem((rank, confs), F32),
            pltpu.SemaphoreType.REGULAR((3,)),
            dma((4,)), dma((4,)), dma((4, chunks)), dma((4, chunks)), dma((1,)), dma((chunks,)),
            dma((1,)), dma((1,)), dma((16,)), dma((16,)), dma((NZ,)), dma((NZ,)), dma((16,)), dma((16,)), dma((16,)), dma((16,)),
            dma((1,)), dma((1,)), dma((16,)), dma((16,)), dma((NZ,)), dma((NZ,)), dma((NZ,)), dma((NZ,)), dma((8,)), dma((8,)),
        ],
        compiler_params=pltpu.CompilerParams(
            collective_id=0, has_side_effects=True, vmem_limit_bytes=60 * 1024 * 1024
        ),
    )(scores, conf_init)


def solution(mesh):
    return jax.shard_map(
        shards,
        mesh=mesh,
        in_specs=(P("hit", "conf"), P("conf", None)),
        out_specs=(P(("hit", "conf"), None), P("conf", None)),
        check_vma=False,
    )
```

```python
import jax
import jax.numpy as jnp
from jax import lax
from jax.experimental import pallas as pl
from jax.experimental.pallas import tpu as pltpu
from jax.sharding import PartitionSpec as P

MESH = pl.DeviceIdType.MESH
F32 = jnp.float32
BF16 = jnp.bfloat16
NX, NZ = 4, 8
CH = 128
PARTS = 4


def exact_dot(a, b):
    return jnp.dot(a, b, precision=lax.Precision.HIGHEST, preferred_element_type=F32)


def split(a):
    high = a.astype(BF16)
    return high, (a - high.astype(F32)).astype(BF16)


def split_dot(a, b):
    (ah, al), (bh, bl) = a, b
    one = lambda u, v: jnp.dot(u, v, preferred_element_type=F32)
    return one(ah, bl) + one(al, bh) + one(ah, bh)


def scaled_steps(low, count):
    scales = []
    for _ in range(count):
        scales.append(2.0 / (1.0 + low))
        low = 4.0 * low / (1.0 + low) ** 2
    return scales


class Inverse:
    def __init__(self, a, low, scaled, corrected):
        n = a.shape[0]
        rows = lax.broadcasted_iota(jnp.int32, (n, n), 0)
        cols = lax.broadcasted_iota(jnp.int32, (n, n), 1)
        self.eye = (rows == cols).astype(F32)
        self.unscale = 1.0 / jnp.sqrt(jnp.sum(a * a, axis=(0, 1), keepdims=True))
        self.a = a * self.unscale
        self.scales = scaled_steps(low, scaled)
        self.corrected = corrected
        s = self.scales[0]
        halves = split(self.a)
        self.x = (2.0 * s) * self.eye - (s * s) * self.a
        self.y = (2.0 * s) * self.a - (s * s) * split_dot(halves, halves)

    def run(self, first, last):
        for s in self.scales[first:last]:
            m = split((2.0 * s) * self.eye - (s * s) * self.y)
            self.x, self.y = split_dot(split(self.x), m), split_dot(split(self.y), m)

    def finish(self):
        x = self.x
        for _ in range(self.corrected):
            x = x + split_dot(split(x), split(self.eye - exact_dot(self.a, x)))
        return x * self.unscale


def kernel(
    ridge_conf,
    ridge_hit,
    scores,
    conf_init,
    hit_out,
    t_full,
    solver_out,
    s_buf,
    c_buf,
    z_buf,
    g_acc,
    t_acc,
    g_core,
    g_half,
    g_xy,
    g_z,
    g_full,
    t_core,
    t_xy,
    t_part,
    t_z,
    known,
    cs, cr, ss, sr, sl, os,
    g1s, g1r, g2s, g2r, g3s, g3r, g4s, g4r, g5s, g5r,
    h1s, h1r, h2s, h2r, h3s, h3r, h4s, h4r, h5s, h5r,
):
    own = s_buf.shape[1]
    chunks = own // CH
    hit = lax.axis_index("hit")
    conf = lax.axis_index("conf")
    x = hit // (2 * NZ)
    z = (hit // 2) % NZ
    yh = hit % 2
    yl = conf // 2
    core = conf % 2

    def device(x_, yh_, z_, yl_, core_):
        return ((x_ * NZ + z_) * 2 + yh_, yl_ * 2 + core_)

    y = yh * 2 + yl
    xy = x * 4 + y

    def along_x(r):
        return device((x + r) % NX, yh, z, yl, core)

    def along_y(r):
        p = (y + r) % 4
        return device(x, p // 2, z, p % 2, core)

    def along_z(r):
        return device(x, yh, (z + r) % NZ, yl, core)

    def xy_peer(r):
        p = (xy + r) % 16
        return p, device(p // 4, (p // 2) % 2, z, p % 2, core)

    group_conf = [conf, yl * 2 + 1 - core, (1 - yl) * 2 + core, (1 - yl) * 2 + 1 - core]
    group = [(hit, c) for c in group_conf]
    beyond = device(x, 1 - yh, z, 1 - yl, core)

    barrier = pltpu.get_barrier_semaphore()
    neighbours = [along_x(1), along_x(3), along_y(1), along_y(3), along_z(1), along_z(NZ - 1)]
    for to in [group[1], group[3]] + neighbours:
        pl.semaphore_signal(barrier, inc=1, device_id=to, device_id_type=MESH)
    pl.semaphore_wait(barrier, 8)

    def tell(k, devices):
        for to in devices:
            pl.semaphore_signal(known.at[k], inc=1, device_id=to, device_id_type=MESH)

    def send(src, dst, send_sem, recv_sem, to):
        return pltpu.make_async_remote_copy(
            src_ref=src, dst_ref=dst, send_sem=send_sem, recv_sem=recv_sem, device_id=to, device_id_type=MESH
        )

    def rows(start, size):
        return pl.ds(pl.multiple_of(start, size), size)

    conf_copies = [send(conf_init, c_buf.at[d], cs.at[d], cr.at[d], to) for d, to in ((1, group[1]), (2, beyond))]
    for copy in conf_copies:
        copy.start()

    def score_copy(d, i):
        return send(
            scores.at[rows(group_conf[d] * own + i * CH, CH)],
            s_buf.at[d, rows(i * CH, CH)],
            ss.at[d, i],
            sr.at[d, i],
            group[d],
        )

    @pl.loop(0, chunks)
    def _(i):
        for d in (2, 3, 1):
            score_copy(d, i).start()

    mine = pltpu.make_async_copy(scores.at[rows(conf * own, own)], s_buf.at[0], sl.at[0])
    mine.start()

    tell(0, neighbours)

    conf_copies[1].wait()
    passed_on = send(c_buf.at[2], c_buf.at[3], cs.at[3], cr.at[3], group[1])
    passed_on.start()
    conf_copies[0].wait()
    c_buf[0] = conf_init[...]
    passed_on.wait()

    def square(m):
        return lax.dot_general(m, m, (((0,), (0,)), ((), ())), preferred_element_type=F32)

    def ridged(gram, ridge):
        n = gram.shape[0]
        r_ = lax.broadcasted_iota(jnp.int32, (n, n), 0)
        c_ = lax.broadcasted_iota(jnp.int32, (n, n), 1)
        return gram + jnp.where(r_ == c_, F32(ridge), F32(0.0))

    gram_conf = (square(c_buf[0]) + square(c_buf[1])) + (square(c_buf[2]) + square(c_buf[3]))
    inverse = Inverse(ridged(gram_conf, ridge_conf), 4.8e-6, 11, 2)
    inverse.run(1, 11)
    g_full[...] = inverse.finish()

    pl.semaphore_wait(known.at[0], 6)
    tell(1, [along_z(2), along_z(NZ - 2)])

    g_acc[...] = jnp.zeros_like(g_acc)
    t_acc[...] = jnp.zeros_like(t_acc)
    mine.wait()

    pl.semaphore_wait(known.at[1], 2)
    tell(2, [along_x(r) for r in (1, 2, 3)])
    pl.semaphore_wait(known.at[2], 3)

    def out_copy(i):
        part = rows(i * CH, CH)
        return pltpu.make_async_copy(z_buf.at[part], hit_out.at[part], os.at[i])

    def solve_chunk(i):
        part = rows(i * CH, CH)
        for d in (1, 2, 3):
            score_copy(d, i).wait()
        rhs = jnp.zeros((CH, 256), F32)
        for d in range(4):
            rhs += jnp.dot(s_buf[d, part, :], c_buf[d], preferred_element_type=F32)
        solved = exact_dot(rhs, g_full[...])
        z_buf[part, :] = solved
        out_copy(i).start()
        turned = solved.T.astype(BF16)
        g_acc[...] += jnp.dot(turned, solved.astype(BF16), preferred_element_type=F32)
        return turned

    def add_cross(i, turned):
        part = rows(i * CH, CH)
        for d in range(4):
            t_acc[d % 2, d // 2] += jnp.dot(turned, s_buf[d, part, :], preferred_element_type=F32)

    @pl.loop(0, chunks - 1)
    def _(i):
        add_cross(i, solve_chunk(i))

    turned = solve_chunk(chunks - 1)

    half = rows(core * 128, 128)
    other_half = rows((1 - core) * 128, 128)
    g1 = send(g_acc.at[other_half], g_core, g1s.at[0], g1r.at[0], group[1])
    g1.start()

    add_cross(chunks - 1, turned)
    h1 = send(t_acc.at[1], t_core, h1s.at[0], h1r.at[0], group[1])
    h1.start()

    g1.wait()
    g_half[...] = g_acc[half, :] + g_core[...]

    def g2(r):
        p, to = xy_peer(r)
        return send(g_half.at[rows(p * 8, 8)], g_xy.at[r], g2s.at[r], g2r.at[r], to)

    @pl.loop(1, 16)
    def _(r):
        g2(r).start()

    h1.wait()
    t_acc[0] += t_core[...]

    def h2(r):
        p, to = xy_peer(r)
        block, part = (p + yl) % 2, p // 4 * 2 + p // 2 % 2
        return send(t_acc.at[0, block, rows(part * 32, 32)], t_xy.at[r], h2s.at[r], h2r.at[r], to)

    @pl.loop(1, 16)
    def _(r):
        h2(r).start()

    g_xy[0] = g_half[rows(xy * 8, 8), :]

    @pl.loop(1, 16)
    def _(r):
        g2(r).wait()

    g_z[z] = jnp.sum(g_xy[...], axis=0)

    def g3(r):
        return send(g_z.at[z], g_z.at[z], g3s.at[r], g3r.at[r], along_z(r))

    @pl.loop(1, NZ)
    def _(r):
        g3(r).start()

    @pl.loop(1, NZ)
    def _(r):
        g3(r).wait()

    def g_rows(p):
        return rows(core * 128 + p * 8, 8)

    g_full[g_rows(xy), :] = jnp.sum(g_z[...], axis=0)

    def g4(r):
        return send(g_full.at[g_rows(xy)], g_full.at[g_rows(xy)], g4s.at[r], g4r.at[r], xy_peer(r)[1])

    def g5(r):
        part = g_rows((xy - r + 16) % 16)
        return send(g_full.at[part], g_full.at[part], g5s.at[r], g5r.at[r], group[1])

    @pl.loop(1, 16)
    def _(r):
        g4(r).start()

    g5(0).start()

    @pl.loop(1, 16)
    def _(r):
        h2(r).wait()

    part = x * 2 + yh
    own_rows = rows(part * 32, 32)
    t_xy[0] = t_acc[0, 0, own_rows, :]
    t_part[...] = jnp.sum(t_xy[...], axis=0)

    def h3(r):
        p = (z + r) % NZ
        tile = t_part.at[rows(p // 2 * 8, 8), rows(p % 2 * 128, 128)]
        return send(tile, t_z.at[r], h3s.at[r], h3r.at[r], along_z(r))

    @pl.loop(1, NZ)
    def _(r):
        h3(r).start()

    t_z[0] = t_part[rows(z // 2 * 8, 8), rows(z % 2 * 128, 128)]

    @pl.loop(1, NZ)
    def _(r):
        h3(r).wait()

    own_tile = (rows(part * 32 + z // 2 * 8, 8), rows(z % 2 * 128, 128))
    t_full[own_tile] = jnp.sum(t_z[...], axis=0)

    def h4(r):
        return send(t_full.at[own_tile], t_full.at[own_tile], h4s.at[r], h4r.at[r], along_z(r))

    @pl.loop(1, NZ)
    def _(r):
        h4(r).start()

    @pl.loop(1, 16)
    def _(r):
        g4(r).wait()
        g5(r).start()

    @pl.loop(0, 16)
    def _(r):
        g5(r).wait()

    inverse = Inverse(ridged(g_full[...], ridge_hit), 4.9e-7, 12, 2)

    @pl.loop(1, NZ)
    def _(r):
        h4(r).wait()

    def h5(r):
        p = (part + r) % 8
        to = device(p // 2, p % 2, z, yl, core)
        return send(t_full.at[own_rows], t_full.at[own_rows], h5s.at[r], h5r.at[r], to)

    @pl.loop(1, 8)
    def _(r):
        h5(r).start()

    inverse.run(1, 12)
    solver_out[...] = inverse.finish()

    @pl.loop(1, 8)
    def _(r):
        h5(r).wait()

    @pl.loop(0, chunks)
    def _(i):
        out_copy(i).wait()


def results(hit_in, rhs_conf, solver, hit_out, conf_out, sems):
    size = hit_in.shape[0] // PARTS
    copies = [
        pltpu.make_async_copy(hit_in.at[pl.ds(i * size, size)], hit_out.at[pl.ds(i * size, size)], sems.at[i])
        for i in range(PARTS)
    ]
    for copy in copies:
        copy.start()
    conf_out[...] = split_dot(split(rhs_conf[...].T), split(solver[...]))
    for copy in copies:
        copy.wait()


def shards(scores, conf_init):
    hits, confs = scores.shape
    rank = conf_init.shape[1]
    own = hits // 4
    chunks = own // CH
    total_hits = hits * lax.axis_size("hit")
    vmem = pltpu.VMEM
    dma = pltpu.SemaphoreType.DMA

    def body(*refs):
        kernel(0.5, 0.5 * total_hits, *refs)

    in_hbm, in_vmem = pl.BlockSpec(memory_space=pl.ANY), pl.BlockSpec(memory_space=pltpu.VMEM)
    hit_factors, rhs_conf, solver = pl.pallas_call(
        body,
        out_shape=(
            jax.ShapeDtypeStruct((own, rank), F32),
            jax.ShapeDtypeStruct((rank, confs), F32),
            jax.ShapeDtypeStruct((rank, rank), F32),
        ),
        in_specs=[in_hbm, in_vmem],
        out_specs=(in_hbm, in_vmem, in_vmem),
        scratch_shapes=[
            vmem((4, own, confs), BF16),
            vmem((4, confs, rank), BF16),
            vmem((own, rank), F32),
            vmem((rank, rank), F32),
            vmem((2, 2, rank, confs), F32),
            vmem((128, rank), F32),
            vmem((128, rank), F32),
            vmem((16, 8, rank), F32),
            vmem((NZ, 8, rank), F32),
            vmem((rank, rank), F32),
            vmem((2, rank, confs), F32),
            vmem((16, 32, confs), F32),
            vmem((32, confs), F32),
            vmem((NZ, 8, 128), F32),
            pltpu.SemaphoreType.REGULAR((3,)),
            dma((4,)), dma((4,)), dma((4, chunks)), dma((4, chunks)), dma((1,)), dma((chunks,)),
            dma((1,)), dma((1,)), dma((16,)), dma((16,)), dma((NZ,)), dma((NZ,)), dma((16,)), dma((16,)), dma((16,)), dma((16,)),
            dma((1,)), dma((1,)), dma((16,)), dma((16,)), dma((NZ,)), dma((NZ,)), dma((NZ,)), dma((NZ,)), dma((8,)), dma((8,)),
        ],
        compiler_params=pltpu.CompilerParams(
            collective_id=0, has_side_effects=True, vmem_limit_bytes=60 * 1024 * 1024
        ),
    )(scores, conf_init)
    return pl.pallas_call(
        results,
        out_shape=(
            jax.ShapeDtypeStruct((own, rank), F32),
            jax.ShapeDtypeStruct((confs, rank), F32),
        ),
        in_specs=[in_hbm, in_vmem, in_vmem],
        out_specs=(in_hbm, in_vmem),
        scratch_shapes=[dma((PARTS,))],
        compiler_params=pltpu.CompilerParams(vmem_limit_bytes=60 * 1024 * 1024),
    )(hit_factors, rhs_conf, solver)


def solution(mesh):
    return jax.shard_map(
        shards,
        mesh=mesh,
        in_specs=(P("hit", "conf"), P("conf", None)),
        out_specs=(P(("hit", "conf"), None), P("conf", None)),
        check_vma=False,
    )
```

```python
import jax
import jax.numpy as jnp
from jax import lax
from jax.experimental import pallas as pl
from jax.experimental.pallas import tpu as pltpu
from jax.sharding import PartitionSpec as P

MESH = pl.DeviceIdType.MESH
F32 = jnp.float32
BF16 = jnp.bfloat16
NX, NZ = 4, 8
CH = 128


def exact_dot(a, b):
    return jnp.dot(a, b, precision=lax.Precision.HIGHEST, preferred_element_type=F32)


def split(a):
    high = a.astype(BF16)
    return high, (a - high.astype(F32)).astype(BF16)


def split_dot(a, b):
    (ah, al), (bh, bl) = a, b
    one = lambda u, v: jnp.dot(u, v, preferred_element_type=F32)
    return one(ah, bl) + one(al, bh) + one(ah, bh)


def scaled_steps(low, count):
    scales = []
    for _ in range(count):
        scales.append(2.0 / (1.0 + low))
        low = 4.0 * low / (1.0 + low) ** 2
    return scales


class Inverse:
    def __init__(self, a, low, scaled, corrected):
        n = a.shape[0]
        rows = lax.broadcasted_iota(jnp.int32, (n, n), 0)
        cols = lax.broadcasted_iota(jnp.int32, (n, n), 1)
        self.eye = (rows == cols).astype(F32)
        self.unscale = 1.0 / jnp.sqrt(jnp.sum(a * a, axis=(0, 1), keepdims=True))
        self.a = a * self.unscale
        self.scales = scaled_steps(low, scaled)
        self.corrected = corrected
        s = self.scales[0]
        halves = split(self.a)
        self.x = (2.0 * s) * self.eye - (s * s) * self.a
        self.y = (2.0 * s) * self.a - (s * s) * split_dot(halves, halves)

    def run(self, first, last):
        for s in self.scales[first:last]:
            m = split((2.0 * s) * self.eye - (s * s) * self.y)
            self.x, self.y = split_dot(split(self.x), m), split_dot(split(self.y), m)

    def finish(self):
        x = self.x
        for _ in range(self.corrected):
            x = x + split_dot(split(x), split(self.eye - exact_dot(self.a, x)))
        return x * self.unscale


def kernel(
    ridge_conf,
    ridge_hit,
    scores,
    conf_init,
    hit_out,
    conf_out,
    s_buf,
    c_buf,
    z_buf,
    g_acc,
    t_acc,
    g_core,
    g_half,
    g_xy,
    g_z,
    g_full,
    t_core,
    t_xy,
    t_part,
    t_z,
    t_full,
    known,
    cs, cr, ss, sr, sl, os,
    g1s, g1r, g2s, g2r, g3s, g3r, g4s, g4r, g5s, g5r,
    h1s, h1r, h2s, h2r, h3s, h3r, h4s, h4r, h5s, h5r,
):
    own = s_buf.shape[1]
    chunks = own // CH
    hit = lax.axis_index("hit")
    conf = lax.axis_index("conf")
    x = hit // (2 * NZ)
    z = (hit // 2) % NZ
    yh = hit % 2
    yl = conf // 2
    core = conf % 2

    def device(x_, yh_, z_, yl_, core_):
        return ((x_ * NZ + z_) * 2 + yh_, yl_ * 2 + core_)

    y = yh * 2 + yl
    xy = x * 4 + y

    def along_x(r):
        return device((x + r) % NX, yh, z, yl, core)

    def along_y(r):
        p = (y + r) % 4
        return device(x, p // 2, z, p % 2, core)

    def along_z(r):
        return device(x, yh, (z + r) % NZ, yl, core)

    def xy_peer(r):
        p = (xy + r) % 16
        return p, device(p // 4, (p // 2) % 2, z, p % 2, core)

    group_conf = [conf, yl * 2 + 1 - core, (1 - yl) * 2 + core, (1 - yl) * 2 + 1 - core]
    group = [(hit, c) for c in group_conf]
    beyond = device(x, 1 - yh, z, 1 - yl, core)

    barrier = pltpu.get_barrier_semaphore()
    neighbours = [along_x(1), along_x(3), along_y(1), along_y(3), along_z(1), along_z(NZ - 1)]
    for to in [group[1], group[3]] + neighbours:
        pl.semaphore_signal(barrier, inc=1, device_id=to, device_id_type=MESH)
    pl.semaphore_wait(barrier, 8)

    def tell(k, devices):
        for to in devices:
            pl.semaphore_signal(known.at[k], inc=1, device_id=to, device_id_type=MESH)

    def send(src, dst, send_sem, recv_sem, to):
        return pltpu.make_async_remote_copy(
            src_ref=src, dst_ref=dst, send_sem=send_sem, recv_sem=recv_sem, device_id=to, device_id_type=MESH
        )

    def rows(start, size):
        return pl.ds(pl.multiple_of(start, size), size)

    conf_copies = [send(conf_init, c_buf.at[d], cs.at[d], cr.at[d], to) for d, to in ((1, group[1]), (2, beyond))]
    for copy in conf_copies:
        copy.start()

    def score_copy(d, i):
        return send(
            scores.at[rows(group_conf[d] * own + i * CH, CH)],
            s_buf.at[d, rows(i * CH, CH)],
            ss.at[d, i],
            sr.at[d, i],
            group[d],
        )

    @pl.loop(0, chunks)
    def _(i):
        for d in (2, 3, 1):
            score_copy(d, i).start()

    mine = pltpu.make_async_copy(scores.at[rows(conf * own, own)], s_buf.at[0], sl.at[0])
    mine.start()

    tell(0, neighbours)

    conf_copies[1].wait()
    passed_on = send(c_buf.at[2], c_buf.at[3], cs.at[3], cr.at[3], group[1])
    passed_on.start()
    conf_copies[0].wait()
    c_buf[0] = conf_init[...]
    passed_on.wait()

    def square(m):
        return lax.dot_general(m, m, (((0,), (0,)), ((), ())), preferred_element_type=F32)

    def ridged(gram, ridge):
        n = gram.shape[0]
        r_ = lax.broadcasted_iota(jnp.int32, (n, n), 0)
        c_ = lax.broadcasted_iota(jnp.int32, (n, n), 1)
        return gram + jnp.where(r_ == c_, F32(ridge), F32(0.0))

    gram_conf = (square(c_buf[0]) + square(c_buf[1])) + (square(c_buf[2]) + square(c_buf[3]))
    inverse = Inverse(ridged(gram_conf, ridge_conf), 4.8e-6, 11, 2)
    inverse.run(1, 11)
    g_full[...] = inverse.finish()

    pl.semaphore_wait(known.at[0], 6)
    tell(1, [along_z(2), along_z(NZ - 2)])

    g_acc[...] = jnp.zeros_like(g_acc)
    t_acc[...] = jnp.zeros_like(t_acc)
    mine.wait()

    pl.semaphore_wait(known.at[1], 2)
    tell(2, [along_x(r) for r in (1, 2, 3)])
    pl.semaphore_wait(known.at[2], 3)

    def out_copy(i):
        part = rows(i * CH, CH)
        return pltpu.make_async_copy(z_buf.at[part], hit_out.at[part], os.at[i])

    def solve_chunk(i):
        part = rows(i * CH, CH)
        for d in (1, 2, 3):
            score_copy(d, i).wait()
        rhs = jnp.zeros((CH, 256), F32)
        for d in range(4):
            rhs += jnp.dot(s_buf[d, part, :], c_buf[d], preferred_element_type=F32)
        solved = exact_dot(rhs, g_full[...])
        z_buf[part, :] = solved
        out_copy(i).start()
        turned = solved.T.astype(BF16)
        g_acc[...] += jnp.dot(turned, solved.astype(BF16), preferred_element_type=F32)
        return turned

    def add_cross(i, turned):
        part = rows(i * CH, CH)
        for d in range(4):
            t_acc[d % 2, d // 2] += jnp.dot(turned, s_buf[d, part, :], preferred_element_type=F32)

    @pl.loop(0, chunks - 1)
    def _(i):
        add_cross(i, solve_chunk(i))

    turned = solve_chunk(chunks - 1)

    half = rows(core * 128, 128)
    other_half = rows((1 - core) * 128, 128)
    g1 = send(g_acc.at[other_half], g_core, g1s.at[0], g1r.at[0], group[1])
    g1.start()

    add_cross(chunks - 1, turned)
    h1 = send(t_acc.at[1], t_core, h1s.at[0], h1r.at[0], group[1])
    h1.start()

    g1.wait()
    g_half[...] = g_acc[half, :] + g_core[...]

    def g2(r):
        p, to = xy_peer(r)
        return send(g_half.at[rows(p * 8, 8)], g_xy.at[r], g2s.at[r], g2r.at[r], to)

    @pl.loop(1, 16)
    def _(r):
        g2(r).start()

    h1.wait()
    t_acc[0] += t_core[...]

    def h2(r):
        p, to = xy_peer(r)
        block, part = (p + yl) % 2, p // 4 * 2 + p // 2 % 2
        return send(t_acc.at[0, block, rows(part * 32, 32)], t_xy.at[r], h2s.at[r], h2r.at[r], to)

    @pl.loop(1, 16)
    def _(r):
        h2(r).start()

    g_xy[0] = g_half[rows(xy * 8, 8), :]

    @pl.loop(1, 16)
    def _(r):
        g2(r).wait()

    g_z[z] = jnp.sum(g_xy[...], axis=0)

    def g3(r):
        return send(g_z.at[z], g_z.at[z], g3s.at[r], g3r.at[r], along_z(r))

    @pl.loop(1, NZ)
    def _(r):
        g3(r).start()

    @pl.loop(1, NZ)
    def _(r):
        g3(r).wait()

    def g_rows(p):
        return rows(core * 128 + p * 8, 8)

    g_full[g_rows(xy), :] = jnp.sum(g_z[...], axis=0)

    def g4(r):
        return send(g_full.at[g_rows(xy)], g_full.at[g_rows(xy)], g4s.at[r], g4r.at[r], xy_peer(r)[1])

    def g5(r):
        part = g_rows((xy - r + 16) % 16)
        return send(g_full.at[part], g_full.at[part], g5s.at[r], g5r.at[r], group[1])

    @pl.loop(1, 16)
    def _(r):
        g4(r).start()

    g5(0).start()

    @pl.loop(1, 16)
    def _(r):
        h2(r).wait()

    part = x * 2 + yh
    own_rows = rows(part * 32, 32)
    t_xy[0] = t_acc[0, 0, own_rows, :]
    t_part[...] = jnp.sum(t_xy[...], axis=0)

    def h3(r):
        p = (z + r) % NZ
        tile = t_part.at[rows(p // 2 * 8, 8), rows(p % 2 * 128, 128)]
        return send(tile, t_z.at[r], h3s.at[r], h3r.at[r], along_z(r))

    @pl.loop(1, NZ)
    def _(r):
        h3(r).start()

    t_z[0] = t_part[rows(z // 2 * 8, 8), rows(z % 2 * 128, 128)]

    @pl.loop(1, NZ)
    def _(r):
        h3(r).wait()

    own_tile = (rows(part * 32 + z // 2 * 8, 8), rows(z % 2 * 128, 128))
    t_full[own_tile] = jnp.sum(t_z[...], axis=0)

    def h4(r):
        return send(t_full.at[own_tile], t_full.at[own_tile], h4s.at[r], h4r.at[r], along_z(r))

    @pl.loop(1, NZ)
    def _(r):
        h4(r).start()

    @pl.loop(1, 16)
    def _(r):
        g4(r).wait()
        g5(r).start()

    @pl.loop(0, 16)
    def _(r):
        g5(r).wait()

    inverse = Inverse(ridged(g_full[...], ridge_hit), 4.9e-7, 12, 2)

    @pl.loop(1, NZ)
    def _(r):
        h4(r).wait()

    def h5(r):
        p = (part + r) % 8
        to = device(p // 2, p % 2, z, yl, core)
        return send(t_full.at[own_rows], t_full.at[own_rows], h5s.at[r], h5r.at[r], to)

    @pl.loop(1, 8)
    def _(r):
        h5(r).start()

    inverse.run(1, 12)
    solver = inverse.finish()

    @pl.loop(1, 8)
    def _(r):
        h5(r).wait()

    conf_out[...] = split_dot(split(t_full[...].T), split(solver))

    @pl.loop(0, chunks)
    def _(i):
        out_copy(i).wait()


def shards(scores, conf_init):
    hits, confs = scores.shape
    rank = conf_init.shape[1]
    own = hits // 4
    chunks = own // CH
    total_hits = hits * lax.axis_size("hit")
    vmem = pltpu.VMEM
    dma = pltpu.SemaphoreType.DMA

    def body(*refs):
        kernel(0.5, 0.5 * total_hits, *refs)

    in_hbm, in_vmem = pl.BlockSpec(memory_space=pl.ANY), pl.BlockSpec(memory_space=pltpu.VMEM)
    return pl.pallas_call(
        body,
        out_shape=(
            jax.ShapeDtypeStruct((own, rank), F32),
            jax.ShapeDtypeStruct((confs, rank), F32),
        ),
        in_specs=[in_hbm, in_vmem],
        out_specs=(in_hbm, in_vmem),
        scratch_shapes=[
            vmem((4, own, confs), BF16),
            vmem((4, confs, rank), BF16),
            vmem((own, rank), F32),
            vmem((rank, rank), F32),
            vmem((2, 2, rank, confs), F32),
            vmem((128, rank), F32),
            vmem((128, rank), F32),
            vmem((16, 8, rank), F32),
            vmem((NZ, 8, rank), F32),
            vmem((rank, rank), F32),
            vmem((2, rank, confs), F32),
            vmem((16, 32, confs), F32),
            vmem((32, confs), F32),
            vmem((NZ, 8, 128), F32),
            vmem((rank, confs), F32),
            pltpu.SemaphoreType.REGULAR((3,)),
            dma((4,)), dma((4,)), dma((4, chunks)), dma((4, chunks)), dma((1,)), dma((chunks,)),
            dma((1,)), dma((1,)), dma((16,)), dma((16,)), dma((NZ,)), dma((NZ,)), dma((16,)), dma((16,)), dma((16,)), dma((16,)),
            dma((1,)), dma((1,)), dma((16,)), dma((16,)), dma((NZ,)), dma((NZ,)), dma((NZ,)), dma((NZ,)), dma((8,)), dma((8,)),
        ],
        compiler_params=pltpu.CompilerParams(
            collective_id=0, has_side_effects=True, vmem_limit_bytes=51 * 1024 * 1024
        ),
    )(scores, conf_init)

def solution(mesh):
    return jax.shard_map(
        shards,
        mesh=mesh,
        in_specs=(P("hit", "conf"), P("conf", None)),
        out_specs=(P(("hit", "conf"), None), P("conf", None)),
        check_vma=False,
    )
```

```python
import jax
import jax.numpy as jnp
from jax import lax
from jax.experimental import pallas as pl
from jax.experimental.pallas import tpu as pltpu
from jax.sharding import PartitionSpec as P

MESH = pl.DeviceIdType.MESH
F32 = jnp.float32
BF16 = jnp.bfloat16
NX, NZ = 4, 8
CH = 128


def exact_dot(a, b):
    return jnp.dot(a, b, precision=lax.Precision.HIGHEST, preferred_element_type=F32)


def split(a):
    high = a.astype(BF16)
    return high, (a - high.astype(F32)).astype(BF16)


def split_dot(a, b):
    (ah, al), (bh, bl) = a, b
    one = lambda u, v: jnp.dot(u, v, preferred_element_type=F32)
    return one(ah, bl) + one(al, bh) + one(ah, bh)


def scaled_steps(low, count):
    scales = []
    for _ in range(count):
        scales.append(2.0 / (1.0 + low))
        low = 4.0 * low / (1.0 + low) ** 2
    return scales


class Inverse:
    def __init__(self, a, low, scaled, corrected):
        n = a.shape[0]
        rows = lax.broadcasted_iota(jnp.int32, (n, n), 0)
        cols = lax.broadcasted_iota(jnp.int32, (n, n), 1)
        self.eye = (rows == cols).astype(F32)
        self.unscale = 1.0 / jnp.sqrt(jnp.sum(a * a, axis=(0, 1), keepdims=True))
        self.a = a * self.unscale
        self.scales = scaled_steps(low, scaled)
        self.corrected = corrected
        s = self.scales[0]
        halves = split(self.a)
        self.x = (2.0 * s) * self.eye - (s * s) * self.a
        self.y = (2.0 * s) * self.a - (s * s) * split_dot(halves, halves)

    def run(self, first, last):
        for s in self.scales[first:last]:
            m = split((2.0 * s) * self.eye - (s * s) * self.y)
            self.x, self.y = split_dot(split(self.x), m), split_dot(split(self.y), m)

    def finish(self):
        x = self.x
        for _ in range(self.corrected):
            x = x + split_dot(split(x), split(self.eye - exact_dot(self.a, x)))
        return x * self.unscale


def kernel(
    ridge_conf,
    ridge_hit,
    scores,
    conf_init,
    hit_out,
    conf_out,
    s_buf,
    c_buf,
    z_buf,
    g_acc,
    t_acc,
    g_core,
    g_half,
    g_xy,
    g_z,
    g_full,
    t_core,
    t_xy,
    t_z,
    t_full,
    known,
    cs, cr, ss, sr, sl, os,
    g1s, g1r, g2s, g2r, g3s, g3r, g4s, g4r, g5s, g5r,
    h1s, h1r, h2s, h2r, h3s, h3r, h4s, h4r,
):
    own = s_buf.shape[1]
    chunks = own // CH
    hit = lax.axis_index("hit")
    conf = lax.axis_index("conf")
    x = hit // (2 * NZ)
    z = (hit // 2) % NZ
    yh = hit % 2
    yl = conf // 2
    core = conf % 2

    def device(x_, yh_, z_, yl_, core_):
        return ((x_ * NZ + z_) * 2 + yh_, yl_ * 2 + core_)

    y = yh * 2 + yl
    xy = x * 4 + y

    def along_x(r):
        return device((x + r) % NX, yh, z, yl, core)

    def along_y(r):
        p = (y + r) % 4
        return device(x, p // 2, z, p % 2, core)

    def along_z(r):
        return device(x, yh, (z + r) % NZ, yl, core)

    def xy_peer(r):
        p = (xy + r) % 16
        return p, device(p // 4, (p // 2) % 2, z, p % 2, core)

    group_conf = [conf, yl * 2 + 1 - core, (1 - yl) * 2 + core, (1 - yl) * 2 + 1 - core]
    group = [(hit, c) for c in group_conf]
    beyond = device(x, 1 - yh, z, 1 - yl, core)

    barrier = pltpu.get_barrier_semaphore()
    neighbours = [along_x(1), along_x(3), along_y(1), along_y(3), along_z(1), along_z(NZ - 1)]
    for to in [group[1], group[3]] + neighbours:
        pl.semaphore_signal(barrier, inc=1, device_id=to, device_id_type=MESH)
    pl.semaphore_wait(barrier, 8)

    def tell(k, devices):
        for to in devices:
            pl.semaphore_signal(known.at[k], inc=1, device_id=to, device_id_type=MESH)

    def send(src, dst, send_sem, recv_sem, to):
        return pltpu.make_async_remote_copy(
            src_ref=src, dst_ref=dst, send_sem=send_sem, recv_sem=recv_sem, device_id=to, device_id_type=MESH
        )

    def rows(start, size):
        return pl.ds(pl.multiple_of(start, size), size)

    conf_copies = [send(conf_init, c_buf.at[d], cs.at[d], cr.at[d], to) for d, to in ((1, group[1]), (2, beyond))]
    for copy in conf_copies:
        copy.start()

    def score_copy(d, i):
        return send(
            scores.at[rows(group_conf[d] * own + i * CH, CH)],
            s_buf.at[d, rows(i * CH, CH)],
            ss.at[d, i],
            sr.at[d, i],
            group[d],
        )

    @pl.loop(0, chunks)
    def _(i):
        for d in (2, 3, 1):
            score_copy(d, i).start()

    mine = pltpu.make_async_copy(scores.at[rows(conf * own, own)], s_buf.at[0], sl.at[0])
    mine.start()

    tell(0, neighbours)

    conf_copies[1].wait()
    passed_on = send(c_buf.at[2], c_buf.at[3], cs.at[3], cr.at[3], group[1])
    passed_on.start()
    conf_copies[0].wait()
    c_buf[0] = conf_init[...]
    passed_on.wait()

    def square(m):
        return lax.dot_general(m, m, (((0,), (0,)), ((), ())), preferred_element_type=F32)

    def ridged(gram, ridge):
        n = gram.shape[0]
        r_ = lax.broadcasted_iota(jnp.int32, (n, n), 0)
        c_ = lax.broadcasted_iota(jnp.int32, (n, n), 1)
        return gram + jnp.where(r_ == c_, F32(ridge), F32(0.0))

    gram_conf = (square(c_buf[0]) + square(c_buf[1])) + (square(c_buf[2]) + square(c_buf[3]))
    inverse = Inverse(ridged(gram_conf, ridge_conf), 4.8e-6, 11, 2)
    inverse.run(1, 11)
    g_full[...] = inverse.finish()

    pl.semaphore_wait(known.at[0], 6)
    tell(1, [along_z(2), along_z(NZ - 2)])

    g_acc[...] = jnp.zeros_like(g_acc)
    t_acc[...] = jnp.zeros_like(t_acc)
    mine.wait()

    pl.semaphore_wait(known.at[1], 2)
    tell(2, [along_x(r) for r in (1, 2, 3)])
    pl.semaphore_wait(known.at[2], 3)

    def out_copy(i):
        part = rows(i * CH, CH)
        return pltpu.make_async_copy(z_buf.at[part], hit_out.at[part], os.at[i])

    def solve_chunk(i):
        part = rows(i * CH, CH)
        for d in (1, 2, 3):
            score_copy(d, i).wait()
        rhs = jnp.zeros((CH, 256), F32)
        for d in range(4):
            rhs += jnp.dot(s_buf[d, part, :], c_buf[d], preferred_element_type=F32)
        solved = exact_dot(rhs, g_full[...])
        z_buf[part, :] = solved
        out_copy(i).start()
        turned = solved.T.astype(BF16)
        g_acc[...] += jnp.dot(turned, solved.astype(BF16), preferred_element_type=F32)
        return turned

    def add_cross(i, turned):
        part = rows(i * CH, CH)
        for d in range(4):
            t_acc[d % 2, d // 2] += jnp.dot(turned, s_buf[d, part, :], preferred_element_type=F32)

    @pl.loop(0, chunks - 1)
    def _(i):
        add_cross(i, solve_chunk(i))

    turned = solve_chunk(chunks - 1)

    half = rows(core * 128, 128)
    other_half = rows((1 - core) * 128, 128)
    g1 = send(g_acc.at[other_half], g_core, g1s.at[0], g1r.at[0], group[1])
    g1.start()

    add_cross(chunks - 1, turned)
    h1 = send(t_acc.at[1], t_core, h1s.at[0], h1r.at[0], group[1])
    h1.start()

    g1.wait()
    g_half[...] = g_acc[half, :] + g_core[...]

    def g2(r):
        p, to = xy_peer(r)
        return send(g_half.at[rows(p * 8, 8)], g_xy.at[r], g2s.at[r], g2r.at[r], to)

    @pl.loop(1, 16)
    def _(r):
        g2(r).start()

    h1.wait()
    t_acc[0] += t_core[...]

    def h2(r):
        p, to = xy_peer(r)
        block, part = (p + yl) % 2, p // 4 * 2 + p // 2 % 2
        return send(t_acc.at[0, block, rows(part * 32, 32)], t_xy.at[r], h2s.at[r], h2r.at[r], to)

    @pl.loop(1, 16)
    def _(r):
        h2(r).start()

    g_xy[0] = g_half[rows(xy * 8, 8), :]

    @pl.loop(1, 16)
    def _(r):
        g2(r).wait()

    g_z[z] = jnp.sum(g_xy[...], axis=0)

    def g3(r):
        return send(g_z.at[z], g_z.at[z], g3s.at[r], g3r.at[r], along_z(r))

    @pl.loop(1, NZ)
    def _(r):
        g3(r).start()

    @pl.loop(1, NZ)
    def _(r):
        g3(r).wait()

    def g_rows(p):
        return rows(core * 128 + p * 8, 8)

    g_full[g_rows(xy), :] = jnp.sum(g_z[...], axis=0)

    def g4(r):
        return send(g_full.at[g_rows(xy)], g_full.at[g_rows(xy)], g4s.at[r], g4r.at[r], xy_peer(r)[1])

    def g5(r):
        part = g_rows((xy - r + 16) % 16)
        return send(g_full.at[part], g_full.at[part], g5s.at[r], g5r.at[r], group[1])

    @pl.loop(1, 16)
    def _(r):
        g4(r).start()

    g5(0).start()

    @pl.loop(1, 16)
    def _(r):
        h2(r).wait()

    part = x * 2 + yh
    own_rows = rows(part * 32, 32)
    t_xy[0] = t_acc[0, 0, own_rows, :]
    t_z[z] = jnp.sum(t_xy[...], axis=0)

    def h3(r):
        return send(t_z.at[z], t_z.at[z], h3s.at[r], h3r.at[r], along_z(r))

    @pl.loop(1, NZ)
    def _(r):
        h3(r).start()

    @pl.loop(1, 16)
    def _(r):
        g4(r).wait()
        g5(r).start()

    @pl.loop(0, 16)
    def _(r):
        g5(r).wait()

    inverse = Inverse(ridged(g_full[...], ridge_hit), 4.9e-7, 11, 2)

    @pl.loop(1, NZ)
    def _(r):
        h3(r).wait()

    t_full[own_rows, :] = jnp.sum(t_z[...], axis=0)

    def h4(r):
        p = (part + r) % 8
        to = device(p // 2, p % 2, z, yl, core)
        return send(t_full.at[own_rows], t_full.at[own_rows], h4s.at[r], h4r.at[r], to)

    @pl.loop(1, 8)
    def _(r):
        h4(r).start()

    inverse.run(1, 11)
    solver = inverse.finish()

    @pl.loop(1, 8)
    def _(r):
        h4(r).wait()

    conf_out[...] = split_dot(split(t_full[...].T), split(solver))

    @pl.loop(0, chunks)
    def _(i):
        out_copy(i).wait()


def shards(scores, conf_init):
    hits, confs = scores.shape
    rank = conf_init.shape[1]
    own = hits // 4
    chunks = own // CH
    total_hits = hits * lax.axis_size("hit")
    vmem = pltpu.VMEM
    dma = pltpu.SemaphoreType.DMA

    def body(*refs):
        kernel(0.5, 0.5 * total_hits, *refs)

    in_hbm, in_vmem = pl.BlockSpec(memory_space=pl.ANY), pl.BlockSpec(memory_space=pltpu.VMEM)
    return pl.pallas_call(
        body,
        out_shape=(
            jax.ShapeDtypeStruct((own, rank), F32),
            jax.ShapeDtypeStruct((confs, rank), F32),
        ),
        in_specs=[in_hbm, in_vmem],
        out_specs=(in_hbm, in_vmem),
        scratch_shapes=[
            vmem((4, own, confs), BF16),
            vmem((4, confs, rank), BF16),
            vmem((own, rank), F32),
            vmem((rank, rank), F32),
            vmem((2, 2, rank, confs), F32),
            vmem((128, rank), F32),
            vmem((128, rank), F32),
            vmem((16, 8, rank), F32),
            vmem((NZ, 8, rank), F32),
            vmem((rank, rank), F32),
            vmem((2, rank, confs), F32),
            vmem((16, 32, confs), F32),
            vmem((NZ, 32, confs), F32),
            vmem((rank, confs), F32),
            pltpu.SemaphoreType.REGULAR((3,)),
            dma((4,)), dma((4,)), dma((4, chunks)), dma((4, chunks)), dma((1,)), dma((chunks,)),
            dma((1,)), dma((1,)), dma((16,)), dma((16,)), dma((NZ,)), dma((NZ,)), dma((16,)), dma((16,)), dma((16,)), dma((16,)),
            dma((1,)), dma((1,)), dma((16,)), dma((16,)), dma((NZ,)), dma((NZ,)), dma((8,)), dma((8,)),
        ],
        compiler_params=pltpu.CompilerParams(
            collective_id=0, has_side_effects=True, vmem_limit_bytes=51 * 1024 * 1024
        ),
    )(scores, conf_init)

def solution(mesh):
    return jax.shard_map(
        shards,
        mesh=mesh,
        in_specs=(P("hit", "conf"), P("conf", None)),
        out_specs=(P(("hit", "conf"), None), P("conf", None)),
        check_vma=False,
    )
```

```python
import jax
import jax.numpy as jnp
from jax import lax
from jax.experimental import pallas as pl
from jax.experimental.pallas import tpu as pltpu
from jax.sharding import PartitionSpec as P

MESH = pl.DeviceIdType.MESH
F32 = jnp.float32
BF16 = jnp.bfloat16
NX, NZ = 4, 8
CH = 128


def exact_dot(a, b):
    return jnp.dot(a, b, precision=lax.Precision.HIGHEST, preferred_element_type=F32)


def split(a):
    high = a.astype(BF16)
    return high, (a - high.astype(F32)).astype(BF16)


def split_dot(a, b):
    (ah, al), (bh, bl) = a, b
    one = lambda u, v: jnp.dot(u, v, preferred_element_type=F32)
    return one(ah, bl) + one(al, bh) + one(ah, bh)


def scaled_steps(low, count):
    scales = []
    for _ in range(count):
        scales.append(2.0 / (1.0 + low))
        low = 4.0 * low / (1.0 + low) ** 2
    return scales


class Inverse:
    def __init__(self, a, low, scaled, corrected):
        n = a.shape[0]
        rows = lax.broadcasted_iota(jnp.int32, (n, n), 0)
        cols = lax.broadcasted_iota(jnp.int32, (n, n), 1)
        self.eye = (rows == cols).astype(F32)
        self.unscale = 1.0 / jnp.sqrt(jnp.sum(a * a, axis=(0, 1), keepdims=True))
        self.a = a * self.unscale
        self.scales = scaled_steps(low, scaled)
        self.corrected = corrected
        s = self.scales[0]
        halves = split(self.a)
        self.x = (2.0 * s) * self.eye - (s * s) * self.a
        self.y = (2.0 * s) * self.a - (s * s) * split_dot(halves, halves)

    def run(self, first, last):
        for s in self.scales[first:last]:
            m = split((2.0 * s) * self.eye - (s * s) * self.y)
            self.x, self.y = split_dot(split(self.x), m), split_dot(split(self.y), m)

    def finish(self):
        x = self.x
        for _ in range(self.corrected):
            x = x + split_dot(split(x), split(self.eye - exact_dot(self.a, x)))
        return x * self.unscale


def kernel(
    ridge_conf,
    ridge_hit,
    scores,
    conf_init,
    hit_out,
    conf_out,
    s_buf,
    c_buf,
    z_buf,
    g_acc,
    t_acc,
    g_core,
    g_half,
    g_xy,
    g_z,
    g_full,
    t_core,
    t_xy,
    t_z,
    t_full,
    known,
    cs, cr, ss, sr, sl, os,
    g1s, g1r, g2s, g2r, g3s, g3r, g4s, g4r, g5s, g5r,
    h1s, h1r, h2s, h2r, h3s, h3r, h4s, h4r,
):
    own = s_buf.shape[1]
    chunks = own // CH
    hit = lax.axis_index("hit")
    conf = lax.axis_index("conf")
    x = hit // (2 * NZ)
    z = (hit // 2) % NZ
    yh = hit % 2
    yl = conf // 2
    core = conf % 2

    def device(x_, yh_, z_, yl_, core_):
        return ((x_ * NZ + z_) * 2 + yh_, yl_ * 2 + core_)

    y = yh * 2 + yl
    xy = x * 4 + y

    def along_x(r):
        return device((x + r) % NX, yh, z, yl, core)

    def along_y(r):
        p = (y + r) % 4
        return device(x, p // 2, z, p % 2, core)

    def along_z(r):
        return device(x, yh, (z + r) % NZ, yl, core)

    def xy_peer(r):
        p = (xy + r) % 16
        return p, device(p // 4, (p // 2) % 2, z, p % 2, core)

    group_conf = [conf, yl * 2 + 1 - core, (1 - yl) * 2 + core, (1 - yl) * 2 + 1 - core]
    group = [(hit, c) for c in group_conf]
    beyond = device(x, 1 - yh, z, 1 - yl, core)

    barrier = pltpu.get_barrier_semaphore()
    neighbours = [along_x(1), along_x(3), along_y(1), along_y(3), along_z(1), along_z(NZ - 1)]
    for to in [group[1], group[3]] + neighbours:
        pl.semaphore_signal(barrier, inc=1, device_id=to, device_id_type=MESH)
    pl.semaphore_wait(barrier, 8)

    def tell(k, devices):
        for to in devices:
            pl.semaphore_signal(known.at[k], inc=1, device_id=to, device_id_type=MESH)

    def send(src, dst, send_sem, recv_sem, to):
        return pltpu.make_async_remote_copy(
            src_ref=src, dst_ref=dst, send_sem=send_sem, recv_sem=recv_sem, device_id=to, device_id_type=MESH
        )

    def rows(start, size):
        return pl.ds(pl.multiple_of(start, size), size)

    conf_copies = [send(conf_init, c_buf.at[d], cs.at[d], cr.at[d], to) for d, to in ((1, group[1]), (2, beyond))]
    for copy in conf_copies:
        copy.start()

    def score_copy(d, i):
        return send(
            scores.at[rows(group_conf[d] * own + i * CH, CH)],
            s_buf.at[d, rows(i * CH, CH)],
            ss.at[d, i],
            sr.at[d, i],
            group[d],
        )

    @pl.loop(0, chunks)
    def _(i):
        for d in (2, 3, 1):
            score_copy(d, i).start()

    mine = pltpu.make_async_copy(scores.at[rows(conf * own, own)], s_buf.at[0], sl.at[0])
    mine.start()

    tell(0, neighbours)

    conf_copies[1].wait()
    passed_on = send(c_buf.at[2], c_buf.at[3], cs.at[3], cr.at[3], group[1])
    passed_on.start()
    conf_copies[0].wait()
    c_buf[0] = conf_init[...]
    passed_on.wait()

    def square(m):
        return lax.dot_general(m, m, (((0,), (0,)), ((), ())), preferred_element_type=F32)

    def ridged(gram, ridge):
        n = gram.shape[0]
        r_ = lax.broadcasted_iota(jnp.int32, (n, n), 0)
        c_ = lax.broadcasted_iota(jnp.int32, (n, n), 1)
        return gram + jnp.where(r_ == c_, F32(ridge), F32(0.0))

    gram_conf = (square(c_buf[0]) + square(c_buf[1])) + (square(c_buf[2]) + square(c_buf[3]))
    inverse = Inverse(ridged(gram_conf, ridge_conf), 4.8e-6, 11, 2)
    inverse.run(1, 11)
    g_full[...] = inverse.finish()

    pl.semaphore_wait(known.at[0], 6)
    tell(1, [along_z(2), along_z(NZ - 2)])

    g_acc[...] = jnp.zeros_like(g_acc)
    t_acc[...] = jnp.zeros_like(t_acc)
    mine.wait()

    pl.semaphore_wait(known.at[1], 2)
    tell(2, [along_x(r) for r in (1, 2, 3)])
    pl.semaphore_wait(known.at[2], 3)

    def out_copy(i):
        part = rows(i * CH, CH)
        return pltpu.make_async_copy(z_buf.at[part], hit_out.at[part], os.at[i])

    def solve_chunk(i):
        part = rows(i * CH, CH)
        for d in (1, 2, 3):
            score_copy(d, i).wait()
        rhs = jnp.zeros((CH, 256), F32)
        for d in range(4):
            rhs += jnp.dot(s_buf[d, part, :], c_buf[d], preferred_element_type=F32)
        solved = exact_dot(rhs, g_full[...])
        z_buf[part, :] = solved
        out_copy(i).start()
        turned = solved.T.astype(BF16)
        g_acc[...] += jnp.dot(turned, solved.astype(BF16), preferred_element_type=F32)
        return turned

    def add_cross(i, turned):
        part = rows(i * CH, CH)
        for d in range(4):
            t_acc[d % 2, d // 2] += jnp.dot(turned, s_buf[d, part, :], preferred_element_type=F32)

    @pl.loop(0, chunks - 1)
    def _(i):
        add_cross(i, solve_chunk(i))

    turned = solve_chunk(chunks - 1)

    half = rows(core * 128, 128)
    other_half = rows((1 - core) * 128, 128)
    g1 = send(g_acc.at[other_half], g_core, g1s.at[0], g1r.at[0], group[1])
    g1.start()

    add_cross(chunks - 1, turned)
    h1 = send(t_acc.at[1], t_core, h1s.at[0], h1r.at[0], group[1])
    h1.start()

    g1.wait()
    g_half[...] = g_acc[half, :] + g_core[...]

    def g2(r):
        p, to = xy_peer(r)
        return send(g_half.at[rows(p * 8, 8)], g_xy.at[r], g2s.at[r], g2r.at[r], to)

    @pl.loop(1, 16)
    def _(r):
        g2(r).start()

    h1.wait()
    t_acc[0] += t_core[...]

    def h2(r):
        p, to = xy_peer(r)
        block, part = (p + yl) % 2, p // 4 * 2 + p // 2 % 2
        return send(t_acc.at[0, block, rows(part * 32, 32)], t_xy.at[r], h2s.at[r], h2r.at[r], to)

    @pl.loop(1, 16)
    def _(r):
        h2(r).start()

    g_xy[0] = g_half[rows(xy * 8, 8), :]

    @pl.loop(1, 16)
    def _(r):
        g2(r).wait()

    g_z[z] = jnp.sum(g_xy[...], axis=0)

    def g3(r):
        return send(g_z.at[z], g_z.at[z], g3s.at[r], g3r.at[r], along_z(r))

    @pl.loop(1, NZ)
    def _(r):
        g3(r).start()

    @pl.loop(1, NZ)
    def _(r):
        g3(r).wait()

    def g_rows(p):
        return rows(core * 128 + p * 8, 8)

    g_full[g_rows(xy), :] = jnp.sum(g_z[...], axis=0)

    def g4(r):
        return send(g_full.at[g_rows(xy)], g_full.at[g_rows(xy)], g4s.at[r], g4r.at[r], xy_peer(r)[1])

    def g5(r):
        part = g_rows((xy - r + 16) % 16)
        return send(g_full.at[part], g_full.at[part], g5s.at[r], g5r.at[r], group[1])

    @pl.loop(1, 16)
    def _(r):
        g4(r).start()

    g5(0).start()

    @pl.loop(1, 16)
    def _(r):
        h2(r).wait()

    part = x * 2 + yh
    own_rows = rows(part * 32, 32)
    t_xy[0] = t_acc[0, 0, own_rows, :]
    t_z[z] = jnp.sum(t_xy[...], axis=0)

    def h3(r):
        return send(t_z.at[z], t_z.at[z], h3s.at[r], h3r.at[r], along_z(r))

    @pl.loop(1, NZ)
    def _(r):
        h3(r).start()

    @pl.loop(1, 16)
    def _(r):
        g4(r).wait()
        g5(r).start()

    @pl.loop(0, 16)
    def _(r):
        g5(r).wait()

    inverse = Inverse(ridged(g_full[...], ridge_hit), 4.9e-7, 12, 2)

    @pl.loop(1, NZ)
    def _(r):
        h3(r).wait()

    t_full[own_rows, :] = jnp.sum(t_z[...], axis=0)

    def h4(r):
        p = (part + r) % 8
        to = device(p // 2, p % 2, z, yl, core)
        return send(t_full.at[own_rows], t_full.at[own_rows], h4s.at[r], h4r.at[r], to)

    @pl.loop(1, 8)
    def _(r):
        h4(r).start()

    inverse.run(1, 12)
    solver = inverse.finish()

    @pl.loop(1, 8)
    def _(r):
        h4(r).wait()

    conf_out[...] = split_dot(split(t_full[...].T), split(solver))

    @pl.loop(0, chunks)
    def _(i):
        out_copy(i).wait()


def shards(scores, conf_init):
    hits, confs = scores.shape
    rank = conf_init.shape[1]
    own = hits // 4
    chunks = own // CH
    total_hits = hits * lax.axis_size("hit")
    vmem = pltpu.VMEM
    dma = pltpu.SemaphoreType.DMA

    def body(*refs):
        kernel(0.5, 0.5 * total_hits, *refs)

    in_hbm, in_vmem = pl.BlockSpec(memory_space=pl.ANY), pl.BlockSpec(memory_space=pltpu.VMEM)
    return pl.pallas_call(
        body,
        out_shape=(
            jax.ShapeDtypeStruct((own, rank), F32),
            jax.ShapeDtypeStruct((confs, rank), F32),
        ),
        in_specs=[in_hbm, in_vmem],
        out_specs=(in_hbm, in_vmem),
        scratch_shapes=[
            vmem((4, own, confs), BF16),
            vmem((4, confs, rank), BF16),
            vmem((own, rank), F32),
            vmem((rank, rank), F32),
            vmem((2, 2, rank, confs), F32),
            vmem((128, rank), F32),
            vmem((128, rank), F32),
            vmem((16, 8, rank), F32),
            vmem((NZ, 8, rank), F32),
            vmem((rank, rank), F32),
            vmem((2, rank, confs), F32),
            vmem((16, 32, confs), F32),
            vmem((NZ, 32, confs), F32),
            vmem((rank, confs), F32),
            pltpu.SemaphoreType.REGULAR((3,)),
            dma((4,)), dma((4,)), dma((4, chunks)), dma((4, chunks)), dma((1,)), dma((chunks,)),
            dma((1,)), dma((1,)), dma((16,)), dma((16,)), dma((NZ,)), dma((NZ,)), dma((16,)), dma((16,)), dma((16,)), dma((16,)),
            dma((1,)), dma((1,)), dma((16,)), dma((16,)), dma((NZ,)), dma((NZ,)), dma((8,)), dma((8,)),
        ],
        compiler_params=pltpu.CompilerParams(
            collective_id=0, has_side_effects=True, vmem_limit_bytes=51 * 1024 * 1024
        ),
    )(scores, conf_init)

def solution(mesh):
    return jax.shard_map(
        shards,
        mesh=mesh,
        in_specs=(P("hit", "conf"), P("conf", None)),
        out_specs=(P(("hit", "conf"), None), P("conf", None)),
        check_vma=False,
    )
```

```python
import jax
import jax.numpy as jnp
from jax import lax
from jax.experimental import pallas as pl
from jax.experimental.pallas import tpu as pltpu
from jax.sharding import PartitionSpec as P

MESH = pl.DeviceIdType.MESH
F32 = jnp.float32
BF16 = jnp.bfloat16
NX, NZ = 4, 8
CH = 128


def exact_dot(a, b):
    return jnp.dot(a, b, precision=lax.Precision.HIGHEST, preferred_element_type=F32)


def split(a):
    high = a.astype(BF16)
    return high, (a - high.astype(F32)).astype(BF16)


def split_dot(a, b):
    (ah, al), (bh, bl) = a, b
    one = lambda u, v: jnp.dot(u, v, preferred_element_type=F32)
    return one(ah, bl) + one(al, bh) + one(ah, bh)


def scaled_steps(low, count):
    scales = []
    for _ in range(count):
        scales.append(2.0 / (1.0 + low))
        low = 4.0 * low / (1.0 + low) ** 2
    return scales


class Inverse:
    def __init__(self, a, low, scaled, corrected):
        n = a.shape[0]
        rows = lax.broadcasted_iota(jnp.int32, (n, n), 0)
        cols = lax.broadcasted_iota(jnp.int32, (n, n), 1)
        self.eye = (rows == cols).astype(F32)
        self.unscale = 1.0 / jnp.sqrt(jnp.sum(a * a, axis=(0, 1), keepdims=True))
        self.a = a * self.unscale
        self.scales = scaled_steps(low, scaled)
        self.corrected = corrected
        s = self.scales[0]
        halves = split(self.a)
        self.x = (2.0 * s) * self.eye - (s * s) * self.a
        self.y = (2.0 * s) * self.a - (s * s) * split_dot(halves, halves)

    def run(self, first, last):
        for s in self.scales[first:last]:
            m = split((2.0 * s) * self.eye - (s * s) * self.y)
            self.x, self.y = split_dot(split(self.x), m), split_dot(split(self.y), m)

    def finish(self):
        x = self.x
        for _ in range(self.corrected):
            x = x + split_dot(split(x), split(self.eye - exact_dot(self.a, x)))
        return x * self.unscale


def kernel(
    ridge_conf,
    ridge_hit,
    scores,
    conf_init,
    hit_out,
    conf_out,
    s_buf,
    c_buf,
    z_buf,
    g_acc,
    t_acc,
    g_core,
    g_half,
    g_xy,
    g_z,
    g_full,
    t_core,
    t_xy,
    t_z,
    t_full,
    g_inv,
    known,
    cs, cr, ss, sr, sl, os,
    g1s, g1r, g2s, g2r, g3s, g3r, g4s, g4r, g5s, g5r,
    h1s, h1r, h2s, h2r, h3s, h3r, h4s, h4r,
):
    own = s_buf.shape[1]
    chunks = own // CH
    hit = lax.axis_index("hit")
    conf = lax.axis_index("conf")
    x = hit // (2 * NZ)
    z = (hit // 2) % NZ
    yh = hit % 2
    yl = conf // 2
    core = conf % 2

    def device(x_, yh_, z_, yl_, core_):
        return ((x_ * NZ + z_) * 2 + yh_, yl_ * 2 + core_)

    y = yh * 2 + yl
    xy = x * 4 + y

    def along_x(r):
        return device((x + r) % NX, yh, z, yl, core)

    def along_y(r):
        p = (y + r) % 4
        return device(x, p // 2, z, p % 2, core)

    def along_z(r):
        return device(x, yh, (z + r) % NZ, yl, core)

    def xy_peer(r):
        p = (xy + r) % 16
        return p, device(p // 4, (p // 2) % 2, z, p % 2, core)

    group_conf = [conf, yl * 2 + 1 - core, (1 - yl) * 2 + core, (1 - yl) * 2 + 1 - core]
    group = [(hit, c) for c in group_conf]
    beyond = device(x, 1 - yh, z, 1 - yl, core)

    barrier = pltpu.get_barrier_semaphore()
    neighbours = [along_x(1), along_x(3), along_y(1), along_y(3), along_z(1), along_z(NZ - 1)]
    for to in [group[1], group[3]] + neighbours:
        pl.semaphore_signal(barrier, inc=1, device_id=to, device_id_type=MESH)
    pl.semaphore_wait(barrier, 8)

    def tell(k, devices):
        for to in devices:
            pl.semaphore_signal(known.at[k], inc=1, device_id=to, device_id_type=MESH)

    def send(src, dst, send_sem, recv_sem, to):
        return pltpu.make_async_remote_copy(
            src_ref=src, dst_ref=dst, send_sem=send_sem, recv_sem=recv_sem, device_id=to, device_id_type=MESH
        )

    def rows(start, size):
        return pl.ds(pl.multiple_of(start, size), size)

    conf_copies = [send(conf_init, c_buf.at[d], cs.at[d], cr.at[d], to) for d, to in ((1, group[1]), (2, beyond))]
    for copy in conf_copies:
        copy.start()

    def score_copy(d, i):
        return send(
            scores.at[rows(group_conf[d] * own + i * CH, CH)],
            s_buf.at[d, rows(i * CH, CH)],
            ss.at[d, i],
            sr.at[d, i],
            group[d],
        )

    @pl.loop(0, chunks)
    def _(i):
        for d in (2, 3, 1):
            score_copy(d, i).start()

    mine = pltpu.make_async_copy(scores.at[rows(conf * own, own)], s_buf.at[0], sl.at[0])
    mine.start()

    tell(0, neighbours)

    conf_copies[1].wait()
    passed_on = send(c_buf.at[2], c_buf.at[3], cs.at[3], cr.at[3], group[1])
    passed_on.start()
    conf_copies[0].wait()
    c_buf[0] = conf_init[...]
    passed_on.wait()

    def square(m):
        return lax.dot_general(m, m, (((0,), (0,)), ((), ())), preferred_element_type=F32)

    def ridged(gram, ridge):
        n = gram.shape[0]
        r_ = lax.broadcasted_iota(jnp.int32, (n, n), 0)
        c_ = lax.broadcasted_iota(jnp.int32, (n, n), 1)
        return gram + jnp.where(r_ == c_, F32(ridge), F32(0.0))

    gram_conf = (square(c_buf[0]) + square(c_buf[1])) + (square(c_buf[2]) + square(c_buf[3]))
    inverse = Inverse(ridged(gram_conf, ridge_conf), 4.8e-6, 11, 2)
    inverse.run(1, 11)
    g_inv[0], g_inv[1] = split(inverse.finish())

    pl.semaphore_wait(known.at[0], 6)
    tell(1, [along_z(2), along_z(NZ - 2)])

    g_acc[...] = jnp.zeros_like(g_acc)
    t_acc[...] = jnp.zeros_like(t_acc)
    mine.wait()

    pl.semaphore_wait(known.at[1], 2)
    tell(2, [along_x(r) for r in (1, 2, 3)])
    pl.semaphore_wait(known.at[2], 3)

    def out_copy(i):
        part = rows(i * CH, CH)
        return pltpu.make_async_copy(z_buf.at[part], hit_out.at[part], os.at[i])

    def solve_chunk(i):
        part = rows(i * CH, CH)
        for d in (1, 2, 3):
            score_copy(d, i).wait()
        rhs = jnp.zeros((CH, 256), F32)
        for d in range(4):
            rhs += jnp.dot(s_buf[d, part, :], c_buf[d], preferred_element_type=F32)
        solved = split_dot(split(rhs), (g_inv[0], g_inv[1]))
        z_buf[part, :] = solved
        out_copy(i).start()
        turned = solved.T.astype(BF16)
        g_acc[...] += jnp.dot(turned, solved.astype(BF16), preferred_element_type=F32)
        return turned

    def add_cross(i, turned):
        part = rows(i * CH, CH)
        for d in range(4):
            t_acc[d % 2, d // 2] += jnp.dot(turned, s_buf[d, part, :], preferred_element_type=F32)

    @pl.loop(0, chunks - 1)
    def _(i):
        add_cross(i, solve_chunk(i))

    turned = solve_chunk(chunks - 1)

    half = rows(core * 128, 128)
    other_half = rows((1 - core) * 128, 128)
    g1 = send(g_acc.at[other_half], g_core, g1s.at[0], g1r.at[0], group[1])
    g1.start()

    add_cross(chunks - 1, turned)
    h1 = send(t_acc.at[1], t_core, h1s.at[0], h1r.at[0], group[1])
    h1.start()

    g1.wait()
    g_half[...] = g_acc[half, :] + g_core[...]

    def g2(r):
        p, to = xy_peer(r)
        return send(g_half.at[rows(p * 8, 8)], g_xy.at[r], g2s.at[r], g2r.at[r], to)

    @pl.loop(1, 16)
    def _(r):
        g2(r).start()

    h1.wait()
    t_acc[0] += t_core[...]

    def h2(r):
        p, to = xy_peer(r)
        block, part = (p + yl) % 2, p // 4 * 2 + p // 2 % 2
        return send(t_acc.at[0, block, rows(part * 32, 32)], t_xy.at[r], h2s.at[r], h2r.at[r], to)

    @pl.loop(1, 16)
    def _(r):
        h2(r).start()

    g_xy[0] = g_half[rows(xy * 8, 8), :]

    @pl.loop(1, 16)
    def _(r):
        g2(r).wait()

    g_z[z] = jnp.sum(g_xy[...], axis=0)

    def g3(r):
        return send(g_z.at[z], g_z.at[z], g3s.at[r], g3r.at[r], along_z(r))

    @pl.loop(1, NZ)
    def _(r):
        g3(r).start()

    @pl.loop(1, NZ)
    def _(r):
        g3(r).wait()

    def g_rows(p):
        return rows(core * 128 + p * 8, 8)

    g_full[g_rows(xy), :] = jnp.sum(g_z[...], axis=0)

    def g4(r):
        return send(g_full.at[g_rows(xy)], g_full.at[g_rows(xy)], g4s.at[r], g4r.at[r], xy_peer(r)[1])

    def g5(r):
        part = g_rows((xy - r + 16) % 16)
        return send(g_full.at[part], g_full.at[part], g5s.at[r], g5r.at[r], group[1])

    @pl.loop(1, 16)
    def _(r):
        g4(r).start()

    g5(0).start()

    @pl.loop(1, 16)
    def _(r):
        h2(r).wait()

    part = x * 2 + yh
    own_rows = rows(part * 32, 32)
    t_xy[0] = t_acc[0, 0, own_rows, :]
    t_z[z] = jnp.sum(t_xy[...], axis=0)

    def h3(r):
        return send(t_z.at[z], t_z.at[z], h3s.at[r], h3r.at[r], along_z(r))

    @pl.loop(1, NZ)
    def _(r):
        h3(r).start()

    @pl.loop(1, 16)
    def _(r):
        g4(r).wait()
        g5(r).start()

    @pl.loop(0, 16)
    def _(r):
        g5(r).wait()

    inverse = Inverse(ridged(g_full[...], ridge_hit), 4.9e-7, 12, 2)

    @pl.loop(1, NZ)
    def _(r):
        h3(r).wait()

    t_full[own_rows, :] = jnp.sum(t_z[...], axis=0)

    def h4(r):
        p = (part + r) % 8
        to = device(p // 2, p % 2, z, yl, core)
        return send(t_full.at[own_rows], t_full.at[own_rows], h4s.at[r], h4r.at[r], to)

    @pl.loop(1, 8)
    def _(r):
        h4(r).start()

    inverse.run(1, 12)
    solver = inverse.finish()

    @pl.loop(1, 8)
    def _(r):
        h4(r).wait()

    conf_out[...] = split_dot(split(t_full[...].T), split(solver))

    @pl.loop(0, chunks)
    def _(i):
        out_copy(i).wait()


def shards(scores, conf_init):
    hits, confs = scores.shape
    rank = conf_init.shape[1]
    own = hits // 4
    chunks = own // CH
    total_hits = hits * lax.axis_size("hit")
    vmem = pltpu.VMEM
    dma = pltpu.SemaphoreType.DMA

    def body(*refs):
        kernel(0.5, 0.5 * total_hits, *refs)

    in_hbm, in_vmem = pl.BlockSpec(memory_space=pl.ANY), pl.BlockSpec(memory_space=pltpu.VMEM)
    return pl.pallas_call(
        body,
        out_shape=(
            jax.ShapeDtypeStruct((own, rank), F32),
            jax.ShapeDtypeStruct((confs, rank), F32),
        ),
        in_specs=[in_hbm, in_vmem],
        out_specs=(in_hbm, in_vmem),
        scratch_shapes=[
            vmem((4, own, confs), BF16),
            vmem((4, confs, rank), BF16),
            vmem((own, rank), F32),
            vmem((rank, rank), F32),
            vmem((2, 2, rank, confs), F32),
            vmem((128, rank), F32),
            vmem((128, rank), F32),
            vmem((16, 8, rank), F32),
            vmem((NZ, 8, rank), F32),
            vmem((rank, rank), F32),
            vmem((2, rank, confs), F32),
            vmem((16, 32, confs), F32),
            vmem((NZ, 32, confs), F32),
            vmem((rank, confs), F32),
            vmem((2, rank, rank), BF16),
            pltpu.SemaphoreType.REGULAR((3,)),
            dma((4,)), dma((4,)), dma((4, chunks)), dma((4, chunks)), dma((1,)), dma((chunks,)),
            dma((1,)), dma((1,)), dma((16,)), dma((16,)), dma((NZ,)), dma((NZ,)), dma((16,)), dma((16,)), dma((16,)), dma((16,)),
            dma((1,)), dma((1,)), dma((16,)), dma((16,)), dma((NZ,)), dma((NZ,)), dma((8,)), dma((8,)),
        ],
        compiler_params=pltpu.CompilerParams(
            collective_id=0, has_side_effects=True, vmem_limit_bytes=51 * 1024 * 1024
        ),
    )(scores, conf_init)

def solution(mesh):
    return jax.shard_map(
        shards,
        mesh=mesh,
        in_specs=(P("hit", "conf"), P("conf", None)),
        out_specs=(P(("hit", "conf"), None), P("conf", None)),
        check_vma=False,
    )
```
